128 devices in a mesh: ctx: 8 (over y_hi, x), head: 16 (over z, y_lo, core).
Axes of the slice: x: 4, y: 4 (y_hi: 2, y_lo: 2; y = y_hi * 2 + y_lo), z: 4, core: 2. Of those that a mesh axis runs over, the one named last changes fastest.
Arguments:
- queries: bfloat16 [4096, 6144], P('ctx', 'head'), may hold values from -6 to 6
- keys: bfloat16 [4096, 6144], P('ctx', 'head'), may hold values from -6 to 6
- values: bfloat16 [4096, 6144], P('ctx', 'head'), may hold values from -6 to 6
- w_out: bfloat16 [6144, 6144], P('head'), may hold values from -0.3125 to 0.3125
- grad_out: bfloat16 [4096, 6144], P(('ctx', 'head')), may hold values from -6 to 6
- slab_order: int32 [16], replicated, may hold values from 0 to 15, each once
- frame_lengths: int32 [16], replicated, may hold values from 1 to 512, 4096 in all
Outputs:
- layer_out: bfloat16 [4096, 6144], P(('ctx', 'head'))
- grad_queries: bfloat16 [4096, 6144], P('ctx', 'head')
- grad_keys: bfloat16 [4096, 6144], P('ctx', 'head')
- grad_values: bfloat16 [4096, 6144], P('ctx', 'head')
The draws below stay inside these ranges and needn't reach their ends.
All inputs are finite; a program needn't handle non-finite values.
Results may differ from the reference program's by a relative error of at most 0.04.
Values may be sent and summed in bfloat16 or wider, within the bound.
No kernel may reach another device: no remote copies, remote signals or barrier semaphores. Data moves between devices by JAX's collectives and lax.ppermute only.
A program may use at most 128 MiB of HBM per device.

```python
import math
import jax
import jax.numpy as jnp
import numpy as np
from jax import lax

D = 6144
HEADS = 48
HD = 128
TOK_DEV = 512
SEQ = 4096
SLAB = 256
SLABS = 16
FRAMES = 16
N_CTX = 8
N_HEAD = 16


def draw_queries(key, part):
    key = jax.random.fold_in(key, 3)
    arr_shape = (SEQ, HEADS * HD)
    base_draw = jnp.clip(1.4 * jax.random.normal(key, arr_shape, jnp.float32), -6.0, 6.0)
    return base_draw.astype(jnp.bfloat16)


def draw_keys(key, part):
    key = jax.random.fold_in(key, 7)
    arr_shape = (SEQ, HEADS * HD)
    base_draw = jnp.clip(1.4 * jax.random.normal(key, arr_shape, jnp.float32), -6.0, 6.0)
    return base_draw.astype(jnp.bfloat16)


def level_of(rng, dims, shards, smallest, high):
    loudness, own = 1.0, jax.random.fold_in(rng, 6)
    for dim, parts in shards:
        heights = jnp.exp(jax.random.uniform(jax.random.fold_in(own, dim), (parts,), jnp.float32, smallest / len(shards), high / len(shards)))
        loudness = loudness * jnp.repeat(heights, dims[dim] // parts).reshape([-1 if axis == dim else 1 for axis in range(len(dims))])
    return loudness


def length_profile(number_of, total, most, skew):
    weights = [(1 << 20) // math.isqrt(grade ** skew) + 1 for grade in range(2, number_of + 1)]
    rest, given = total - most - (number_of - 1), [1] * (number_of - 1)
    while rest > 0:
        candidates = [i for i in range(number_of - 1) if given[i] < most]
        pool, budget = sum([weights[i] for i in candidates]), rest
        for i in candidates:
            more = min(most - given[i], max(1, budget * weights[i] // pool), rest)
            given[i] = given[i] + more
            rest = rest - more
    return np.array([most] + given)


def ragged(rng, number_of, total, most, lean):
    if number_of == 2:
        one = jax.random.randint(rng, (), max(1, total - most), min(most, total - 1) + 1)
        return jnp.stack([one, total - one])
    lengths = jnp.asarray(length_profile(number_of, total, most, lean), jnp.int32)
    pairs = (number_of - 1) // 2
    donor, receiver = lengths[1:1 + 2 * pairs:2], lengths[2:2 + 2 * pairs:2]
    slack = jnp.minimum(donor - 1, most - receiver)
    moved = jax.random.randint(jax.random.fold_in(rng, 1), (pairs,), 0, 1 << 20) % (slack + 1)
    lengths = lengths.at[1:1 + 2 * pairs:2].set(donor - moved).at[2:2 + 2 * pairs:2].set(receiver + moved)
    return lengths[jax.random.permutation(jax.random.fold_in(rng, 2), number_of)]


def normal_values(stream_key, extent, scale, most, split=(), kind=jnp.bfloat16):
    entries = jax.random.normal(stream_key, extent, jnp.float32) * scale
    if len(split) > 0:
        entries = level_of(stream_key, extent, split, -0.22, 0.18) * entries
    return jnp.clip(entries, min=-most, max=most).astype(kind)


def setup_inputs(seed: int = 0) -> dict:
    splits = jax.random.split(jax.random.key(seed), 8)
    queries = draw_queries(jax.random.fold_in(splits[7], 71), 0)
    keys = draw_keys(jax.random.fold_in(splits[7], 71), 0)
    values = normal_values(splits[2], (SEQ, HEADS * HD), 1.0, 6.0, ((0, 8), (1, 16)))
    w_out = normal_values(splits[3], (HEADS * HD, D), (HEADS * HD // 16) ** -0.5, 0.3125, ((0, 16),))
    grad_out = normal_values(splits[4], (SEQ, D), 1.0, 6.0, ((0, 128),))
    slab_order = jax.random.permutation(splits[5], SLABS).astype(jnp.int32)
    frame_lengths = ragged(splits[6], FRAMES, SEQ, TOK_DEV, 2).astype(jnp.int32)
    return {"queries": queries, "keys": keys, "values": values, "w_out": w_out, "grad_out": grad_out, "slab_order": slab_order, "frame_lengths": frame_lengths}


def frame_ids(slab_order, frame_lengths):
    row_index = jnp.arange(SEQ, dtype=jnp.int32)
    position = slab_order[row_index // SLAB].astype(jnp.int32) * SLAB + row_index % SLAB
    frame_ends = jnp.cumsum(frame_lengths).astype(jnp.int32)
    return jnp.sum((frame_ends[None, :] <= position[:, None]).astype(jnp.int32), axis=1)


def settle(partial_sum):
    return lax.optimization_barrier(partial_sum.astype(jnp.bfloat16)).astype(jnp.float32)


def reference(queries, keys, values, w_out, grad_out, slab_order, frame_lengths):
    frames = frame_ids(slab_order, frame_lengths)
    visible = frames[None, :] <= frames[:, None]
    scale_factor = float(HD) ** -0.5
    grad_mixed = jnp.dot(grad_out, w_out.T, preferred_element_type=jnp.float32).astype(jnp.bfloat16)

    def to_heads(matrix):
        return matrix.reshape(SEQ, HEADS, HD).transpose(1, 0, 2)

    def from_heads(stacked):
        return stacked.transpose(1, 0, 2).reshape(SEQ, HEADS * HD)

    def one_head(inputs):
        query_head, key_head, value_head, dout_head = inputs
        score_tile = jnp.dot(query_head, key_head.T, preferred_element_type=jnp.float32) * scale_factor
        score_tile = jnp.where(visible, score_tile, -jnp.inf)
        log_total = jax.nn.logsumexp(score_tile, axis=1)
        weights = jnp.exp(score_tile - log_total[:, None])
        weights_low = weights.astype(jnp.bfloat16)
        mixed_head = jnp.dot(weights_low, value_head, preferred_element_type=jnp.float32).astype(jnp.bfloat16)
        row_dot = jnp.sum(dout_head.astype(jnp.float32) * mixed_head.astype(jnp.float32), axis=1)
        d_weights = jnp.dot(dout_head, value_head.T, preferred_element_type=jnp.float32)
        d_scores = (weights * (d_weights - row_dot[:, None])).astype(jnp.bfloat16)
        q_grad = (jnp.dot(d_scores, key_head, preferred_element_type=jnp.float32) * scale_factor).astype(jnp.bfloat16)
        score_blocks = d_scores.astype(jnp.float32).reshape(N_CTX, TOK_DEV, SEQ)
        weight_blocks = weights_low.astype(jnp.float32).reshape(N_CTX, TOK_DEV, SEQ)
        query_rows = query_head.astype(jnp.float32).reshape(N_CTX, TOK_DEV, HD)
        dout_rows = dout_head.astype(jnp.float32).reshape(N_CTX, TOK_DEV, HD)
        key_parts = settle(jnp.einsum("cqk,cqd->ckd", score_blocks, query_rows))
        value_parts = settle(jnp.einsum("cqk,cqd->ckd", weight_blocks, dout_rows))
        k_grad = (jnp.sum(key_parts, axis=0) * scale_factor).astype(jnp.bfloat16)
        v_grad = jnp.sum(value_parts, axis=0).astype(jnp.bfloat16)
        return mixed_head, q_grad, k_grad, v_grad

    mixed_all, q_all, k_all, v_all = lax.map(one_head, (to_heads(queries), to_heads(keys), to_heads(values), to_heads(grad_mixed)))
    group_width = (HEADS // N_HEAD) * HD
    mixed_groups = from_heads(mixed_all).reshape(SEQ, N_HEAD, group_width).transpose(1, 0, 2)
    weight_groups = w_out.reshape(N_HEAD, group_width, D)

    def add_group(total, pair):
        mixed_group, weight_group = pair
        return total + settle(jnp.dot(mixed_group, weight_group, preferred_element_type=jnp.float32)), None

    out_total, _ = lax.scan(add_group, jnp.zeros((SEQ, D), jnp.float32), (mixed_groups, weight_groups))
    layer_out = out_total.astype(jnp.bfloat16)
    return layer_out, from_heads(q_all), from_heads(k_all), from_heads(v_all)
```

```python
import functools
import math

import jax
import jax.numpy as jnp
from jax import lax
from jax.experimental import pallas as pl
from jax.experimental.pallas import tpu as pltpu
from jax.sharding import PartitionSpec as P

HD = 128
LOG2E = math.log2(math.e)
SCALE = float(HD) ** -0.5
SCALE2 = SCALE * LOG2E
START_MAX = -1e20
HIDDEN = -1e30
F32, BF16 = jnp.float32, jnp.bfloat16
NT = (((1,), (1,)), ((), ()))
TN = (((0,), (0,)), ((), ()))
NN = (((1,), (0,)), ((), ()))


def dot(a, b, dims):
    return lax.dot_general(a, b, dims, preferred_element_type=F32)


def last_visible(ends, pos):
    limit = ends[-1]
    for end in reversed(ends[:-1]):
        limit = jnp.where(end > pos, end, limit)
    return limit


def visibility(place_ref, order_ref, length_ref, limit_ref, span_ref, base_ref, slab, n_query, n_key):
    ends, total = [], jnp.int32(0)
    for f in range(length_ref.shape[0]):
        total = total + length_ref[f]
        ends.append(total)
    for i in range(n_query):
        base = order_ref[place_ref[i // 2] * 2 + i % 2] * slab
        rows = base + lax.broadcasted_iota(jnp.int32, (1, slab), 1)
        limit_ref[:, i * slab : (i + 1) * slab] = last_visible(ends, rows)
        span_ref[i, 0] = last_visible(ends, base)
        span_ref[i, 1] = last_visible(ends, base + slab - 1)
    for j in range(n_key):
        base_ref[j] = order_ref[place_ref[2 + j // 2] * 2 + j % 2] * slab


def for_pairs(body, limit_ref, span_ref, base_ref, slab, n_query, n_key):
    def step(t, carry):
        j, i = t // n_query, t % n_query
        base = base_ref[j]
        low, high = span_ref[i, 0], span_ref[i, 1]

        @pl.when(base + slab <= low)
        def _():
            body(i, j, None)

        @pl.when(jnp.logical_and(base < high, base + slab > low))
        def _():
            limit = limit_ref[:, pl.ds(pl.multiple_of(i * slab, slab), slab)] - base
            body(i, j, lax.broadcasted_iota(jnp.int32, (slab, slab), 0) >= limit)

        return carry

    lax.fori_loop(0, n_query * n_key, step, 0)


def forward_kernel(blocks, heads, slab, *refs):
    place_ref, order_ref, length_ref, *refs = refs
    query_refs, refs = refs[:2], refs[2:]
    kv_refs, refs = refs[:blocks], refs[blocks:]
    own_ref, own_lse_ref, peer_ref, peer_lse_ref, *refs = refs
    q_ref, k_ref, v_ref, acc_ref, max_ref, sum_ref, limit_ref, span_ref, base_ref = refs
    n_query, n_key = 4, 2 * blocks
    rows, width = 2 * slab, heads * HD
    visibility(place_ref, order_ref, length_ref, limit_ref, span_ref, base_ref, slab, n_query, n_key)
    for b in range(2):
        q_ref[b * rows : (b + 1) * rows, :] = query_refs[b][...]
    for b in range(blocks):
        k_ref[b * rows : (b + 1) * rows, :] = kv_refs[b][:, :width]
        v_ref[b * rows : (b + 1) * rows, :] = kv_refs[b][:, width:]
    acc_ref[...] = jnp.zeros_like(acc_ref)
    max_ref[...] = jnp.full_like(max_ref, START_MAX)
    sum_ref[...] = jnp.zeros_like(sum_ref)

    def body(i, j, hidden):
        q_rows = pl.ds(pl.multiple_of(i * slab, slab), slab)
        k_rows = pl.ds(pl.multiple_of(j * slab, slab), slab)
        for h in range(heads):
            cols = slice(h * HD, (h + 1) * HD)
            score = dot(k_ref[k_rows, cols], q_ref[q_rows, cols], NT) * SCALE2
            if hidden is not None:
                score = jnp.where(hidden, HIDDEN, score)
            old = max_ref[h : h + 1, q_rows]
            new = jnp.maximum(old, jnp.max(score, axis=0, keepdims=True))
            weight = jnp.exp2(score - new)
            fade = jnp.exp2(old - new)
            max_ref[h : h + 1, q_rows] = new
            sum_ref[h : h + 1, q_rows] = sum_ref[h : h + 1, q_rows] * fade + jnp.sum(
                weight, axis=0, keepdims=True
            )
            acc_ref[cols, q_rows] = acc_ref[cols, q_rows] * fade + dot(
                v_ref[k_rows, cols], weight.astype(BF16), TN
            )

    for_pairs(body, limit_ref, span_ref, base_ref, slab, n_query, n_key)
    total = jnp.maximum(sum_ref[...], 1e-30)
    lse = max_ref[...] + jnp.log2(total)
    own_lse_ref[...] = lse[:, :rows]
    peer_lse_ref[...] = lse[:, rows:]
    for b, out_ref in enumerate((own_ref, peer_ref)):
        for s in range(2):
            at = slice((2 * b + s) * slab, (2 * b + s + 1) * slab)
            for h in range(heads):
                cols = slice(h * HD, (h + 1) * HD)
                mixed = acc_ref[cols, at] / total[h : h + 1, at]
                out_ref[s * slab : (s + 1) * slab, cols] = mixed.T.astype(out_ref.dtype)


def merge_kernel(heads, slab, own_ref, own_lse_ref, from_ref, from_lse_ref, mixed_ref, lse_ref):
    a, b = own_lse_ref[...], from_lse_ref[...]
    top = jnp.maximum(a, b)
    lse = top + jnp.log2(jnp.exp2(a - top) + jnp.exp2(b - top))
    lse_ref[...] = lse
    share_a, share_b = jnp.exp2(a - lse), jnp.exp2(b - lse)
    for s in range(2):
        at = slice(s * slab, (s + 1) * slab)
        for h in range(heads):
            cols = slice(h * HD, (h + 1) * HD)
            wa = jnp.broadcast_to(share_a[h : h + 1, at], (HD, slab)).T
            wb = jnp.broadcast_to(share_b[h : h + 1, at], (HD, slab)).T
            mixed_ref[at, cols] = (
                own_ref[at, cols] * wa + from_ref[at, cols].astype(F32) * wb
            ).astype(BF16)


def stats_kernel(heads, slab, mixed_ref, dout_ref, lse_ref, stats_ref):
    stats_ref[...] = lse_ref[...]
    for s in range(2):
        at = slice(s * slab, (s + 1) * slab)
        for h in range(heads):
            cols = slice(h * HD, (h + 1) * HD)
            prod = mixed_ref[at, cols].astype(F32) * dout_ref[at, cols].astype(F32)
            stats_ref[heads + h : heads + h + 1, at] = jnp.sum(prod.T, axis=0, keepdims=True)


def backward_kernel(blocks, heads, slab, *refs):
    place_ref, order_ref, length_ref, *refs = refs
    query_refs, dout_refs, stat_refs, refs = refs[:2], refs[2:4], refs[4:6], refs[6:]
    kv_refs, refs = refs[:blocks], refs[blocks:]
    own_ref, peer_ref, *refs = refs
    dkv_refs, refs = refs[:blocks], refs[blocks:]
    q_ref, do_ref, k_ref, v_ref, dq_ref, dk_ref, dv_ref, stat_ref, limit_ref, span_ref, base_ref = refs
    n_query, n_key = 4, 2 * blocks
    rows, width = 2 * slab, heads * HD
    visibility(place_ref, order_ref, length_ref, limit_ref, span_ref, base_ref, slab, n_query, n_key)
    for b in range(2):
        at = slice(b * rows, (b + 1) * rows)
        q_ref[at, :] = query_refs[b][...]
        do_ref[at, :] = dout_refs[b][...]
        stat_ref[:, at] = stat_refs[b][...]
    for b in range(blocks):
        k_ref[b * rows : (b + 1) * rows, :] = kv_refs[b][:, :width]
        v_ref[b * rows : (b + 1) * rows, :] = kv_refs[b][:, width:]
    dq_ref[...] = jnp.zeros_like(dq_ref)
    dk_ref[...] = jnp.zeros_like(dk_ref)
    dv_ref[...] = jnp.zeros_like(dv_ref)

    def body(i, j, hidden):
        q_rows = pl.ds(pl.multiple_of(i * slab, slab), slab)
        k_rows = pl.ds(pl.multiple_of(j * slab, slab), slab)
        for h in range(heads):
            cols = slice(h * HD, (h + 1) * HD)
            query, dout = q_ref[q_rows, cols], do_ref[q_rows, cols]
            key = k_ref[k_rows, cols]
            score = dot(key, query, NT) * SCALE2
            weight = jnp.exp2(score - stat_ref[h : h + 1, q_rows])
            if hidden is not None:
                weight = jnp.where(hidden, 0.0, weight)
            d_weight = dot(v_ref[k_rows, cols], dout, NT)
            d_score = (weight * (d_weight - stat_ref[heads + h : heads + h + 1, q_rows])).astype(BF16)
            dv_ref[k_rows, cols] += dot(weight.astype(BF16), dout, NN)
            dk_ref[k_rows, cols] += dot(d_score, query, NN)
            dq_ref[cols, q_rows] += dot(key, d_score, TN)

    for_pairs(body, limit_ref, span_ref, base_ref, slab, n_query, n_key)
    for b, out_ref in enumerate((own_ref, peer_ref)):
        for s in range(2):
            at = slice((2 * b + s) * slab, (2 * b + s + 1) * slab)
            for h in range(heads):
                cols = slice(h * HD, (h + 1) * HD)
                out_ref[s * slab : (s + 1) * slab, cols] = (dq_ref[cols, at] * SCALE).T.astype(out_ref.dtype)
    for b in range(blocks):
        at = slice(b * rows, (b + 1) * rows)
        dkv_refs[b][:, :width] = (dk_ref[at, :] * SCALE).astype(BF16)
        dkv_refs[b][:, width:] = dv_ref[at, :].astype(BF16)


SMEM = pl.BlockSpec(memory_space=pltpu.SMEM)
VMEM = pl.BlockSpec(memory_space=pltpu.VMEM)
LIMIT = 40 * 2**20


def call(kernel, outs, n_scalar, n_vector, scratch, name, flops):
    return pl.pallas_call(
        kernel,
        out_shape=[jax.ShapeDtypeStruct(shape, dtype) for shape, dtype in outs],
        in_specs=[SMEM] * n_scalar + [VMEM] * n_vector,
        out_specs=[VMEM] * len(outs),
        scratch_shapes=scratch,
        compiler_params=pltpu.CompilerParams(vmem_limit_bytes=LIMIT),
        cost_estimate=pl.CostEstimate(flops=flops, bytes_accessed=4 << 20, transcendentals=0),
        name=name,
    )


def on_device(queries, keys, values, w_out, grad_out, slab_order, frame_lengths):
    rows, width = queries.shape
    heads, slab = width // HD, rows // 2
    n_head = lax.axis_size("head")
    half = w_out.shape[1] // 2
    ctx, head = lax.axis_index("ctx"), lax.axis_index("head")
    core = head % 2

    def over_x(array, o):
        perm = [(y * 4 + x, y * 4 + (x - o) % 4) for y in range(2) for x in range(4)]
        return lax.ppermute(array, "ctx", perm)

    def over_y(array):
        return lax.ppermute(array, "ctx", [(c, (c + 4) % 8) for c in range(8)])

    def over_core(array):
        return lax.ppermute(array, "head", [(h, h ^ 1) for h in range(n_head)])

    def over_chips(array, dz, dy):
        perm = [(h, ((h // 4 + dz) % 4) * 4 + (h ^ (2 * dy)) % 4) for h in range(n_head)]
        return lax.ppermute(array, "head", perm)

    offsets = (2, 1, 3, 0)
    place = jnp.stack([ctx, (ctx + 4) % 8] + [ctx // 4 * 4 + (ctx + o) % 4 for o in offsets])
    place = place.astype(jnp.int32)
    scalars = (place, slab_order, frame_lengths)

    peer_queries = over_y(queries)
    kv = jnp.concatenate([keys, values], axis=1)
    kv_blocks = [over_x(kv, o) if o else kv for o in offsets]
    grad_rows = lax.all_gather(grad_out, "head", axis=0, tiled=True)
    w_here = jnp.where(core == 0, w_out[:, :half], w_out[:, half:])
    w_there = over_core(jnp.where(core == 0, w_out[:, half:], w_out[:, :half]))
    w_pair = jnp.concatenate([w_here, w_there], axis=0)

    n_block = len(offsets)
    part = (rows, width)
    stat = (8, rows)
    work = 2 * 2 * rows * n_block * rows * width
    masks = [
        pltpu.VMEM((1, 2 * rows), jnp.int32),
        pltpu.SMEM((4, 2), jnp.int32),
        pltpu.SMEM((2 * n_block,), jnp.int32),
    ]
    own_mixed, own_lse, peer_mixed, peer_lse = call(
        functools.partial(forward_kernel, n_block, heads, slab),
        [(part, F32), (stat, F32), (part, BF16), (stat, F32)],
        3,
        2 + n_block,
        [
            pltpu.VMEM((2 * rows, width), BF16),
            pltpu.VMEM((n_block * rows, width), BF16),
            pltpu.VMEM((n_block * rows, width), BF16),
            pltpu.VMEM((width, 2 * rows), F32),
            pltpu.VMEM((8, 2 * rows), F32),
            pltpu.VMEM((8, 2 * rows), F32),
        ]
        + masks,
        "forward",
        2 * work,
    )(*scalars, queries, peer_queries, *kv_blocks)

    mixed, lse = call(
        functools.partial(merge_kernel, heads, slab),
        [(part, BF16), (stat, F32)],
        0,
        4,
        [],
        "merge",
        1 << 20,
    )(own_mixed, own_lse, over_y(peer_mixed), over_y(peer_lse))

    grad_mixed = lax.dot_general(grad_rows, w_out, NT, preferred_element_type=F32).astype(BF16)
    peer_grad = over_y(grad_mixed)
    (stats,) = call(
        functools.partial(stats_kernel, heads, slab), [(stat, F32)], 0, 3, [], "stats", 1 << 20
    )(mixed, grad_mixed, lse)
    peer_stats = over_y(stats)

    pair = jnp.concatenate([mixed, over_core(mixed)], axis=1)
    out_part = jnp.dot(pair, w_pair, preferred_element_type=F32).astype(BF16)
    chip_rows = 2 * rows // n_head
    chip = head // 2
    total = lax.dynamic_slice_in_dim(out_part, chip * chip_rows, chip_rows).astype(F32)
    for dz, dy in ((2, 1), (2, 0), (1, 1), (3, 1), (1, 0), (3, 0), (0, 1)):
        target = ((chip // 2 + dz) % 4) * 2 + (chip + dy) % 2
        piece = lax.dynamic_slice_in_dim(out_part, target * chip_rows, chip_rows)
        total = total + over_chips(piece, dz, dy).astype(F32)
    total = total.astype(BF16).reshape(2, chip_rows // 2, half)
    mine = jnp.where(core == 0, total[0], total[1])
    other = over_core(jnp.where(core == 0, total[1], total[0]))
    layer_out = jnp.concatenate(
        [jnp.where(core == 0, mine, other), jnp.where(core == 0, other, mine)], axis=1
    )

    own_dq, peer_dq, *dkv = call(
        functools.partial(backward_kernel, n_block, heads, slab),
        [(part, F32), (part, BF16)] + [((rows, 2 * width), BF16)] * n_block,
        3,
        6 + n_block,
        [
            pltpu.VMEM((2 * rows, width), BF16),
            pltpu.VMEM((2 * rows, width), BF16),
            pltpu.VMEM((n_block * rows, width), BF16),
            pltpu.VMEM((n_block * rows, width), BF16),
            pltpu.VMEM((width, 2 * rows), F32),
            pltpu.VMEM((n_block * rows, width), F32),
            pltpu.VMEM((n_block * rows, width), F32),
            pltpu.VMEM((8, 2 * rows), F32),
        ]
        + masks,
        "backward",
        5 * work,
    )(*scalars, queries, peer_queries, grad_mixed, peer_grad, stats, peer_stats, *kv_blocks)
    q_grad = (own_dq + over_y(peer_dq).astype(F32)).astype(BF16)
    kv_grad = sum(over_x(d, (4 - o) % 4).astype(F32) if o else d.astype(F32) for d, o in zip(dkv, offsets))
    kv_grad = kv_grad.astype(BF16)
    return layer_out, q_grad, kv_grad[:, :width], kv_grad[:, width:]


def solution(mesh):
    in_specs = (
        P("ctx", "head"),
        P("ctx", "head"),
        P("ctx", "head"),
        P("head", None),
        P(("ctx", "head"), None),
        P(),
        P(),
    )
    out_specs = (P(("ctx", "head"), None), P("ctx", "head"), P("ctx", "head"), P("ctx", "head"))
    return jax.shard_map(on_device, mesh=mesh, in_specs=in_specs, out_specs=out_specs, check_vma=False)
```

```python
import functools
import math

import jax
import jax.numpy as jnp
from jax import lax
from jax.experimental import pallas as pl
from jax.experimental.pallas import tpu as pltpu
from jax.sharding import PartitionSpec as P

HD = 128
LOG2E = math.log2(math.e)
SCALE = float(HD) ** -0.5
SCALE2 = SCALE * LOG2E
START_MAX = -1e20
HIDDEN = -1e30
F32, BF16 = jnp.float32, jnp.bfloat16
NT = (((1,), (1,)), ((), ()))
TN = (((0,), (0,)), ((), ()))
NN = (((1,), (0,)), ((), ()))


def dot(a, b, dims):
    return lax.dot_general(a, b, dims, preferred_element_type=F32)


def last_visible(ends, pos):
    limit = ends[-1]
    for end in reversed(ends[:-1]):
        limit = jnp.where(end > pos, end, limit)
    return limit


def visibility(facts_ref, limit_ref, span_ref, base_ref, slab, keys):
    n_slot = 8
    order, length = 2 + n_slot, 2 + n_slot + (facts_ref.shape[0] - 2 - n_slot) // 2
    ends, total = [], jnp.int32(0)
    for f in range(length, facts_ref.shape[0]):
        total = total + facts_ref[f]
        ends.append(total)
    for i in range(4):
        base = facts_ref[order + facts_ref[i // 2] * 2 + i % 2] * slab
        rows = base + lax.broadcasted_iota(jnp.int32, (1, slab), 1)
        limit_ref[:, i * slab : (i + 1) * slab] = last_visible(ends, rows)
        span_ref[i, 0] = last_visible(ends, base)
        span_ref[i, 1] = last_visible(ends, base + slab - 1)
    for j, key in enumerate(keys):
        base_ref[j] = facts_ref[order + facts_ref[2 + key]] * slab


def for_pairs(body, limit_ref, span_ref, base_ref, slab, n_key):
    for j in range(n_key):
        for b in range(2):

            def step(i, carry, b=b, j=j):
                base = base_ref[j]
                low, high = span_ref[2 * b + i, 0], span_ref[2 * b + i, 1]
                q_rows = pl.ds(pl.multiple_of(i * slab, slab), slab)
                all_rows = pl.ds(pl.multiple_of((2 * b + i) * slab, slab), slab)

                @pl.when(base + slab <= low)
                def _():
                    body(b, j, q_rows, all_rows, None)

                @pl.when(jnp.logical_and(base < high, base + slab > low))
                def _():
                    limit = limit_ref[:, all_rows] - base
                    hidden = lax.broadcasted_iota(jnp.int32, (slab, slab), 0) >= limit
                    body(b, j, q_rows, all_rows, hidden)

                return carry

            lax.fori_loop(0, 2, step, 0)


def forward_kernel(keys, heads, slab, first, last, *refs):
    facts_ref, *refs = refs
    n_key = len(keys)
    query_refs, refs = refs[:2], refs[2:]
    kv_refs, refs = refs[:n_key], refs[n_key:]
    state_refs, refs = ([], refs) if first else (refs[:3], refs[3:])
    if last:
        own_ref, own_lse_ref, peer_ref, peer_lse_ref, *refs = refs
    acc_ref, max_ref, sum_ref, limit_ref, span_ref, base_ref = refs
    rows, width = 2 * slab, heads * HD
    visibility(facts_ref, limit_ref, span_ref, base_ref, slab, keys)
    if first:
        acc_ref[...] = jnp.zeros_like(acc_ref)
        max_ref[...] = jnp.full_like(max_ref, START_MAX)
        sum_ref[...] = jnp.zeros_like(sum_ref)
    else:
        for to_ref, from_ref in zip((acc_ref, max_ref, sum_ref), state_refs):
            to_ref[...] = from_ref[...]

    def body(b, j, q_rows, all_rows, hidden):
        every = [slice(h * HD, (h + 1) * HD) for h in range(heads)]
        key = [kv_refs[j][:, cols] for cols in every]
        value = [kv_refs[j][:, width + h * HD : width + (h + 1) * HD] for h in range(heads)]
        old = [max_ref[h : h + 1, all_rows] for h in range(heads)]
        scores = [dot(key[h], query_refs[b][q_rows, cols], NT) * SCALE2 for h, cols in enumerate(every)]
        if hidden is not None:
            scores = [jnp.where(hidden, HIDDEN, score) for score in scores]
        new = [jnp.maximum(m, jnp.max(x, axis=0, keepdims=True)) for m, x in zip(old, scores)]
        weights = [jnp.exp2(x - m) for x, m in zip(scores, new)]
        fades = [jnp.exp2(m - n) for m, n in zip(old, new)]
        sums = [
            sum_ref[h : h + 1, all_rows] * fades[h] + jnp.sum(weights[h], axis=0, keepdims=True)
            for h in range(heads)
        ]
        mixes = [dot(v, w.astype(BF16), TN) for v, w in zip(value, weights)]
        for h, cols in enumerate(every):
            max_ref[h : h + 1, all_rows] = new[h]
            sum_ref[h : h + 1, all_rows] = sums[h]
            acc_ref[cols, all_rows] = acc_ref[cols, all_rows] * fades[h] + mixes[h]

    for_pairs(body, limit_ref, span_ref, base_ref, slab, n_key)
    if not last:
        return
    total = jnp.maximum(sum_ref[...], 1e-30)
    lse = max_ref[...] + jnp.log2(total)
    own_lse_ref[...] = lse[:, :rows]
    peer_lse_ref[...] = lse[:, rows:]
    for b, out_ref in enumerate((own_ref, peer_ref)):
        for s in range(2):
            at = slice((2 * b + s) * slab, (2 * b + s + 1) * slab)
            for h in range(heads):
                cols = slice(h * HD, (h + 1) * HD)
                mixed = acc_ref[cols, at] / total[h : h + 1, at]
                out_ref[s * slab : (s + 1) * slab, cols] = mixed.T.astype(out_ref.dtype)


def merge_kernel(heads, slab, own_ref, own_lse_ref, from_ref, from_lse_ref, mixed_ref, lse_ref):
    a, b = own_lse_ref[...], from_lse_ref[...]
    top = jnp.maximum(a, b)
    lse = top + jnp.log2(jnp.exp2(a - top) + jnp.exp2(b - top))
    lse_ref[...] = lse
    share_a, share_b = jnp.exp2(a - lse), jnp.exp2(b - lse)
    for s in range(2):
        at = slice(s * slab, (s + 1) * slab)
        for h in range(heads):
            cols = slice(h * HD, (h + 1) * HD)
            wa = jnp.broadcast_to(share_a[h : h + 1, at], (HD, slab)).T
            wb = jnp.broadcast_to(share_b[h : h + 1, at], (HD, slab)).T
            mixed_ref[at, cols] = (
                own_ref[at, cols] * wa + from_ref[at, cols].astype(F32) * wb
            ).astype(BF16)


def stats_kernel(heads, slab, mixed_ref, dout_ref, lse_ref, stats_ref):
    stats_ref[...] = lse_ref[...]
    for s in range(2):
        at = slice(s * slab, (s + 1) * slab)
        for h in range(heads):
            cols = slice(h * HD, (h + 1) * HD)
            prod = mixed_ref[at, cols].astype(F32) * dout_ref[at, cols].astype(F32)
            stats_ref[heads + h : heads + h + 1, at] = jnp.sum(prod.T, axis=0, keepdims=True)


def backward_kernel(keys, heads, slab, first, last, *refs):
    facts_ref, *refs = refs
    n_key = len(keys)
    query_refs, dout_refs, stat_refs, refs = refs[:2], refs[2:4], refs[4:6], refs[6:]
    kv_refs, refs = refs[:n_key], refs[n_key:]
    state_refs, refs = ([], refs) if first else (refs[:1], refs[1:])
    dkv_refs, refs = refs[: n_key // 2], refs[n_key // 2 :]
    if last:
        own_ref, peer_ref, *refs = refs
    dq_ref, dk_ref, dv_ref, limit_ref, span_ref, base_ref = refs
    rows, width = 2 * slab, heads * HD
    visibility(facts_ref, limit_ref, span_ref, base_ref, slab, keys)
    if first:
        dq_ref[...] = jnp.zeros_like(dq_ref)
    else:
        dq_ref[...] = state_refs[0][...]
    dk_ref[...] = jnp.zeros_like(dk_ref)
    dv_ref[...] = jnp.zeros_like(dv_ref)

    def body(b, j, q_rows, all_rows, hidden):
        every = [slice(h * HD, (h + 1) * HD) for h in range(heads)]
        query = [query_refs[b][q_rows, cols] for cols in every]
        dout = [dout_refs[b][q_rows, cols] for cols in every]
        lse = [stat_refs[b][h : h + 1, q_rows] for h in range(heads)]
        row_dot = [stat_refs[b][heads + h : heads + h + 1, q_rows] for h in range(heads)]
        key = [kv_refs[j][:, cols] for cols in every]
        value = [kv_refs[j][:, width + h * HD : width + (h + 1) * HD] for h in range(heads)]
        scores = [dot(key[h], query[h], NT) * SCALE2 for h in range(heads)]
        weights = [jnp.exp2(scores[h] - lse[h]) for h in range(heads)]
        if hidden is not None:
            weights = [jnp.where(hidden, 0.0, weight) for weight in weights]
        d_weights = [dot(value[h], dout[h], NT) for h in range(heads)]
        d_scores = [(weights[h] * (d_weights[h] - row_dot[h])).astype(BF16) for h in range(heads)]
        add_v = [dot(weights[h].astype(BF16), dout[h], NN) for h in range(heads)]
        add_k = [dot(d_scores[h], query[h], NN) for h in range(heads)]
        add_q = [dot(key[h], d_scores[h], TN) for h in range(heads)]
        for h, cols in enumerate(every):
            dv_ref[j, :, cols] += add_v[h]
            dk_ref[j, :, cols] += add_k[h]
            dq_ref[cols, all_rows] += add_q[h]

    for_pairs(body, limit_ref, span_ref, base_ref, slab, n_key)
    for j in range(n_key):
        at = slice(j % 2 * slab, (j % 2 + 1) * slab)
        dkv_refs[j // 2][at, :width] = (dk_ref[j] * SCALE).astype(BF16)
        dkv_refs[j // 2][at, width:] = dv_ref[j].astype(BF16)
    if not last:
        return
    for b, out_ref in enumerate((own_ref, peer_ref)):
        for s in range(2):
            at = slice((2 * b + s) * slab, (2 * b + s + 1) * slab)
            for h in range(heads):
                cols = slice(h * HD, (h + 1) * HD)
                out_ref[s * slab : (s + 1) * slab, cols] = (dq_ref[cols, at] * SCALE).T.astype(out_ref.dtype)


def grad_kernel(steps, grad_hbm, w_hbm, out_ref, grad_ref, w_ref, grad_sem, w_sem):
    tile = grad_ref.shape[2]
    copies = []
    for k in range(steps):
        at = pl.ds(k * tile, tile)
        copies.append(
            (
                pltpu.make_async_copy(grad_hbm.at[:, at], grad_ref.at[k], grad_sem.at[k]),
                pltpu.make_async_copy(w_hbm.at[:, at], w_ref.at[k], w_sem.at[k]),
            )
        )
        for copy in copies[-1]:
            copy.start()
    total = None
    for k in range(steps):
        for copy in copies[k]:
            copy.wait()
        part = dot(grad_ref[k], w_ref[k], NT)
        total = part if total is None else total + part
    out_ref[...] = total.astype(BF16)


def project_grad(grad_rows, w_out, tile):
    rows, width, steps = grad_rows.shape[0], w_out.shape[0], w_out.shape[1] // tile
    hbm = pl.BlockSpec(memory_space=pltpu.MemorySpace.HBM)
    return pl.pallas_call(
        functools.partial(grad_kernel, steps),
        out_shape=jax.ShapeDtypeStruct((rows, width), BF16),
        in_specs=[hbm, hbm],
        out_specs=VMEM,
        scratch_shapes=[
            pltpu.VMEM((steps, rows, tile), BF16),
            pltpu.VMEM((steps, width, tile), BF16),
            pltpu.SemaphoreType.DMA((steps,)),
            pltpu.SemaphoreType.DMA((steps,)),
        ],
        compiler_params=pltpu.CompilerParams(vmem_limit_bytes=20 * 2**20),
        cost_estimate=CHEAP,
        name="project_grad",
    )(grad_rows, w_out)


def out_kernel(core_ref, mixed_ref, other_ref, w_here_ref, w_there_ref, out_ref, pair_ref, w_ref):
    width = mixed_ref.shape[1]

    @pl.when(pl.program_id(0) == 0)
    def _():
        pair_ref[:, :width] = mixed_ref[...]
        pair_ref[:, width:] = other_ref[...]

    w_ref[:width, :] = w_here_ref[...]
    w_ref[width:, :] = w_there_ref[...]
    out_ref[...] = dot(pair_ref[...], w_ref[...], NN).astype(BF16)


def project_out(core, mixed, other, w_out, w_there, tile):
    (rows, width), half = mixed.shape, w_there.shape[1]
    return pl.pallas_call(
        out_kernel,
        grid_spec=pltpu.PrefetchScalarGridSpec(
            num_scalar_prefetch=1,
            grid=(half // tile,),
            in_specs=[
                pl.BlockSpec((rows, width), lambda n, c: (0, 0)),
                pl.BlockSpec((rows, width), lambda n, c: (0, 0)),
                pl.BlockSpec((width, tile), lambda n, c: (0, c[0] * (half // tile) + n)),
                pl.BlockSpec((width, tile), lambda n, c: (0, n)),
            ],
            out_specs=pl.BlockSpec((rows, tile), lambda n, c: (0, n)),
            scratch_shapes=[pltpu.VMEM((rows, 2 * width), BF16), pltpu.VMEM((2 * width, tile), BF16)],
        ),
        out_shape=jax.ShapeDtypeStruct((rows, half), BF16),
        compiler_params=pltpu.CompilerParams(vmem_limit_bytes=LIMIT),
        cost_estimate=CHEAP,
        name="project_out",
    )(core.reshape(1).astype(jnp.int32), mixed, other, w_out, w_there)


CHEAP = pl.CostEstimate(flops=1, bytes_accessed=1, transcendentals=0)
SMEM = pl.BlockSpec(memory_space=pltpu.SMEM)
VMEM = pl.BlockSpec(memory_space=pltpu.VMEM)
LIMIT = 16 * 2**20


def call(kernel, outs, n_scalar, n_vector, scratch, name):
    return pl.pallas_call(
        kernel,
        out_shape=[jax.ShapeDtypeStruct(shape, dtype) for shape, dtype in outs],
        in_specs=[SMEM] * n_scalar + [VMEM] * n_vector,
        out_specs=[VMEM] * len(outs),
        scratch_shapes=scratch,
        compiler_params=pltpu.CompilerParams(vmem_limit_bytes=LIMIT),
        cost_estimate=CHEAP,
        name=name,
    )


def on_device(queries, keys, values, w_out, grad_out, slab_order, frame_lengths):
    rows, width = queries.shape
    heads, slab = width // HD, rows // 2
    n_head = lax.axis_size("head")
    half = w_out.shape[1] // 2
    ctx, head = lax.axis_index("ctx"), lax.axis_index("head")
    core = head % 2

    def over_x(array, o):
        perm = [(y * 4 + x, y * 4 + (x - o) % 4) for y in range(2) for x in range(4)]
        return lax.ppermute(array, "ctx", perm)

    def over_y(array):
        return lax.ppermute(array, "ctx", [(c, (c + 4) % 8) for c in range(8)])

    def over_core(array):
        return lax.ppermute(array, "head", [(h, h ^ 1) for h in range(n_head)])

    def over_chips(array, dz, dy):
        perm = [(h, ((h // 4 + dz) % 4) * 4 + (h ^ (2 * dy)) % 4) for h in range(n_head)]
        return lax.ppermute(array, "head", perm)

    offsets = (0, 1, 3, 2)
    base = ctx // 4 * 4
    slots = [(base + (ctx + o) % 4) * 2 + s for o in offsets for s in range(2)]
    places = jnp.stack([ctx, (ctx + 4) % 8] + slots).astype(jnp.int32)
    facts = jnp.concatenate([places, slab_order, frame_lengths])
    part = (rows, width)
    stat = (8, rows)

    def masks(n_key):
        return [
            pltpu.VMEM((1, 2 * rows), jnp.int32),
            pltpu.SMEM((4, 2), jnp.int32),
            pltpu.SMEM((n_key,), jnp.int32),
        ]

    def forward(keys, state, last):
        n_key = len(keys)
        states = [((width, 2 * rows), F32), ((8, 2 * rows), F32), ((8, 2 * rows), F32)]
        results = [(part, F32), (stat, F32), (part, BF16), (stat, F32)]
        return call(
            functools.partial(forward_kernel, keys, heads, slab, not state, last),
            results if last else states,
            1,
            2 + n_key + len(state),
            [pltpu.VMEM(*s) for s in states if last] + masks(n_key),
            "forward",
        )(facts, queries, peer_queries, *(kv[k] for k in keys), *state)

    def backward(keys, state, last):
        n_key, n_block = len(keys), len(keys) // 2
        states = [((width, 2 * rows), F32)]
        results = [(part, F32), (part, BF16)]
        scratch = [
            pltpu.VMEM((n_key, slab, width), F32),
            pltpu.VMEM((n_key, slab, width), F32),
        ]
        outs = call(
            functools.partial(backward_kernel, keys, heads, slab, not state, last),
            [((rows, 2 * width), BF16)] * n_block + (results if last else states),
            1,
            6 + n_key + len(state),
            [pltpu.VMEM(*s) for s in states if last] + scratch + masks(n_key),
            "backward",
        )(
            facts,
            queries,
            peer_queries,
            grad_mixed,
            peer_grad,
            stats,
            peer_stats,
            *(kv[k] for k in keys),
            *state,
        )
        return outs[:n_block], outs[n_block:]

    peer_queries = over_y(queries)
    kv = [jnp.concatenate([keys[at], values[at]], axis=1) for at in (slice(0, slab), slice(slab, rows))]
    next_0, prev_1 = over_x(kv[0], 1), over_x(kv[1], 3)
    next_1, prev_0 = over_x(kv[1], 1), over_x(kv[0], 3)
    kv += [next_0, next_1, prev_0, prev_1, over_x(next_0, 1), over_x(prev_1, 3)]
    grad_rows = lax.all_gather(grad_out, "head", axis=0, tiled=True)

    w_there = over_core(lax.dynamic_slice_in_dim(w_out, (1 - core) * half, half, 1))
    w_there, kv[2] = lax.optimization_barrier((w_there, kv[2]))
    state = forward((0, 1, 2, 5), [], False)
    own_mixed, own_lse, peer_mixed, peer_lse = forward((3, 4, 6, 7), state, True)
    from_lse, from_mixed = over_y(peer_lse), over_y(peer_mixed)

    grad_rows, peer_lse = lax.optimization_barrier((grad_rows, peer_lse))
    grad_mixed = project_grad(grad_rows, w_out, 1024)
    peer_grad = over_y(grad_mixed)
    from_mixed, grad_mixed = lax.optimization_barrier((from_mixed, grad_mixed))

    mixed, lse = call(
        functools.partial(merge_kernel, heads, slab),
        [(part, BF16), (stat, F32)],
        0,
        4,
        [],
        "merge",
    )(own_mixed, own_lse, from_mixed, from_lse)
    (stats,) = call(
        functools.partial(stats_kernel, heads, slab), [(stat, F32)], 0, 3, [], "stats"
    )(mixed, grad_mixed, lse)
    peer_stats = over_y(stats)

    out_part = project_out(core, mixed, over_core(mixed), w_out, w_there, 512)
    z_groups = [[z * 4 + r for z in range(4)] for r in range(4)]
    out_part, peer_grad, peer_stats = lax.optimization_barrier((out_part, peer_grad, peer_stats))
    out_rows = lax.psum_scatter(
        out_part, "head", scatter_dimension=0, tiled=True, axis_index_groups=z_groups
    )

    (far_dkv,), state = backward((6, 7), [], False)
    far_dkv = over_x(far_dkv, 2)
    (own_dkv,), state = backward((0, 1), state, False)
    (next_dkv, prev_dkv), (own_dq, peer_dq) = backward((2, 3, 4, 5), state, True)
    next_dkv, prev_dkv = over_x(next_dkv, 3), over_x(prev_dkv, 1)
    peer_dq = over_y(peer_dq)

    own_dkv, far_dkv = lax.optimization_barrier((own_dkv, far_dkv))
    kv_early = own_dkv.astype(F32) + far_dkv.astype(F32)
    kv_early, next_dkv, prev_dkv, peer_dq = lax.optimization_barrier((kv_early, next_dkv, prev_dkv, peer_dq))
    kv_grad = (kv_early + next_dkv.astype(F32) + prev_dkv.astype(F32)).astype(BF16)
    q_grad = (own_dq + peer_dq.astype(F32)).astype(BF16)

    few = 2 * rows // n_head // 2
    y_lo = head // 2 % 2
    to_send = lax.dynamic_slice_in_dim(out_rows, (1 - y_lo) * 2 * few, 2 * few)
    total = lax.dynamic_slice_in_dim(out_rows, y_lo * 2 * few, 2 * few).astype(F32)
    received = over_chips(to_send, 0, 1)
    received, kv_grad, q_grad = lax.optimization_barrier((received, kv_grad, q_grad))
    total = (total + received.astype(F32)).astype(BF16).reshape(2, few, half)
    here = jnp.where(core == 0, total[0], total[1])
    there = over_core(jnp.where(core == 0, total[1], total[0]))
    layer_out = jnp.concatenate(
        [jnp.where(core == 0, here, there), jnp.where(core == 0, there, here)], axis=1
    )
    return layer_out, q_grad, kv_grad[:, :width], kv_grad[:, width:]


def solution(mesh):
    in_specs = (
        P("ctx", "head"),
        P("ctx", "head"),
        P("ctx", "head"),
        P("head", None),
        P(("ctx", "head"), None),
        P(),
        P(),
    )
    out_specs = (P(("ctx", "head"), None), P("ctx", "head"), P("ctx", "head"), P("ctx", "head"))
    return jax.shard_map(on_device, mesh=mesh, in_specs=in_specs, out_specs=out_specs, check_vma=False)
```

```python
import functools
import math

import jax
import jax.numpy as jnp
from jax import lax
from jax.experimental import pallas as pl
from jax.experimental.pallas import tpu as pltpu
from jax.sharding import PartitionSpec as P

HD = 128
LOG2E = math.log2(math.e)
SCALE = float(HD) ** -0.5
SCALE2 = SCALE * LOG2E
START_MAX = -1e20
HIDDEN = -1e30
F32, BF16 = jnp.float32, jnp.bfloat16
NT = (((1,), (1,)), ((), ()))
TN = (((0,), (0,)), ((), ()))
NN = (((1,), (0,)), ((), ()))


def in_hbm(array):
    return pltpu.with_memory_space_constraint(array, pltpu.MemorySpace.HBM)


def dot(a, b, dims):
    return lax.dot_general(a, b, dims, preferred_element_type=F32)


def last_visible(ends, pos):
    limit = ends[-1]
    for end in reversed(ends[:-1]):
        limit = jnp.where(end > pos, end, limit)
    return limit


def visibility(facts_ref, limit_ref, span_ref, base_ref, slab, keys):
    n_slot = 8
    order, length = 2 + n_slot, 2 + n_slot + (facts_ref.shape[0] - 2 - n_slot) // 2
    ends, total = [], jnp.int32(0)
    for f in range(length, facts_ref.shape[0]):
        total = total + facts_ref[f]
        ends.append(total)
    for i in range(4):
        base = facts_ref[order + facts_ref[i // 2] * 2 + i % 2] * slab
        rows = base + lax.broadcasted_iota(jnp.int32, (1, slab), 1)
        limit_ref[:, i * slab : (i + 1) * slab] = last_visible(ends, rows)
        span_ref[i, 0] = last_visible(ends, base)
        span_ref[i, 1] = last_visible(ends, base + slab - 1)
    for j, key in enumerate(keys):
        base_ref[j] = facts_ref[order + facts_ref[2 + key]] * slab


def for_pairs(body, limit_ref, span_ref, base_ref, slab, pairs):
    for j, b in pairs:

        def step(i, carry, b=b, j=j):
            base = base_ref[j]
            low, high = span_ref[2 * b + i, 0], span_ref[2 * b + i, 1]
            q_rows = pl.ds(pl.multiple_of(i * slab, slab), slab)
            all_rows = pl.ds(pl.multiple_of((2 * b + i) * slab, slab), slab)

            @pl.when(base + slab <= low)
            def _():
                body(b, j, q_rows, all_rows, None)

            @pl.when(jnp.logical_and(base < high, base + slab > low))
            def _():
                limit = limit_ref[:, all_rows] - base
                hidden = lax.broadcasted_iota(jnp.int32, (slab, slab), 0) >= limit
                body(b, j, q_rows, all_rows, hidden)

            return carry

        lax.fori_loop(0, 2, step, 0)


def forward_kernel(keys, pairs, heads, slab, first, last, *refs):
    facts_ref, *refs = refs
    n_key = len(keys)
    n_query = 1 + max(b for _, b in pairs)
    query_refs, refs = refs[:n_query], refs[n_query:]
    kv_refs, refs = refs[:n_key], refs[n_key:]
    state_refs, refs = ([], refs) if first else (refs[:3], refs[3:])
    if last:
        own_ref, own_lse_ref, peer_ref, peer_lse_ref, *refs = refs
    acc_ref, max_ref, sum_ref, limit_ref, span_ref, base_ref = refs
    rows, width = 2 * slab, heads * HD
    visibility(facts_ref, limit_ref, span_ref, base_ref, slab, keys)
    if first:
        acc_ref[...] = jnp.zeros_like(acc_ref)
        max_ref[...] = jnp.full_like(max_ref, START_MAX)
        sum_ref[...] = jnp.zeros_like(sum_ref)
    else:
        for to_ref, from_ref in zip((acc_ref, max_ref, sum_ref), state_refs):
            to_ref[...] = from_ref[...]

    def body(b, j, q_rows, all_rows, hidden):
        every = [slice(h * HD, (h + 1) * HD) for h in range(heads)]
        key = [kv_refs[j][:, cols] for cols in every]
        value = [kv_refs[j][:, width + h * HD : width + (h + 1) * HD] for h in range(heads)]
        old = [max_ref[h : h + 1, all_rows] for h in range(heads)]
        scores = [dot(key[h], query_refs[b][q_rows, cols], NT) * SCALE2 for h, cols in enumerate(every)]
        if hidden is not None:
            scores = [jnp.where(hidden, HIDDEN, score) for score in scores]
        new = [jnp.maximum(m, jnp.max(x, axis=0, keepdims=True)) for m, x in zip(old, scores)]
        weights = [jnp.exp2(x - m) for x, m in zip(scores, new)]
        fades = [jnp.exp2(m - n) for m, n in zip(old, new)]
        sums = [
            sum_ref[h : h + 1, all_rows] * fades[h] + jnp.sum(weights[h], axis=0, keepdims=True)
            for h in range(heads)
        ]
        mixes = [dot(v, w.astype(BF16), TN) for v, w in zip(value, weights)]
        for h, cols in enumerate(every):
            max_ref[h : h + 1, all_rows] = new[h]
            sum_ref[h : h + 1, all_rows] = sums[h]
            acc_ref[cols, all_rows] = acc_ref[cols, all_rows] * fades[h] + mixes[h]

    for_pairs(body, limit_ref, span_ref, base_ref, slab, pairs)
    if not last:
        return
    total = jnp.maximum(sum_ref[...], 1e-30)
    lse = max_ref[...] + jnp.log2(total)
    own_lse_ref[...] = lse[:, :rows]
    peer_lse_ref[...] = lse[:, rows:]
    for b, out_ref in enumerate((own_ref, peer_ref)):
        for s in range(2):
            at = slice((2 * b + s) * slab, (2 * b + s + 1) * slab)
            for h in range(heads):
                cols = slice(h * HD, (h + 1) * HD)
                mixed = acc_ref[cols, at] / total[h : h + 1, at]
                out_ref[s * slab : (s + 1) * slab, cols] = mixed.T.astype(out_ref.dtype)


def merge_kernel(heads, slab, own_ref, own_lse_ref, from_ref, from_lse_ref, mixed_ref, lse_ref):
    a, b = own_lse_ref[...], from_lse_ref[...]
    top = jnp.maximum(a, b)
    lse = top + jnp.log2(jnp.exp2(a - top) + jnp.exp2(b - top))
    lse_ref[...] = lse
    share_a, share_b = jnp.exp2(a - lse), jnp.exp2(b - lse)
    for s in range(2):
        at = slice(s * slab, (s + 1) * slab)
        for h in range(heads):
            cols = slice(h * HD, (h + 1) * HD)
            wa = jnp.broadcast_to(share_a[h : h + 1, at], (HD, slab)).T
            wb = jnp.broadcast_to(share_b[h : h + 1, at], (HD, slab)).T
            mixed_ref[at, cols] = (
                own_ref[at, cols] * wa + from_ref[at, cols].astype(F32) * wb
            ).astype(BF16)


def stats_kernel(heads, slab, mixed_ref, dout_ref, lse_ref, stats_ref):
    stats_ref[...] = lse_ref[...]
    for s in range(2):
        at = slice(s * slab, (s + 1) * slab)
        for h in range(heads):
            cols = slice(h * HD, (h + 1) * HD)
            prod = mixed_ref[at, cols].astype(F32) * dout_ref[at, cols].astype(F32)
            stats_ref[heads + h : heads + h + 1, at] = jnp.sum(prod.T, axis=0, keepdims=True)


def backward_kernel(keys, heads, slab, first, last, *refs):
    facts_ref, *refs = refs
    n_key = len(keys)
    query_refs, dout_refs, stat_refs, refs = refs[:2], refs[2:4], refs[4:6], refs[6:]
    kv_refs, refs = refs[:n_key], refs[n_key:]
    state_refs, refs = ([], refs) if first else (refs[:1], refs[1:])
    dkv_refs, refs = refs[: n_key // 2], refs[n_key // 2 :]
    if last:
        own_ref, peer_ref, *refs = refs
    dq_ref, dk_ref, dv_ref, limit_ref, span_ref, base_ref = refs
    rows, width = 2 * slab, heads * HD
    visibility(facts_ref, limit_ref, span_ref, base_ref, slab, keys)
    if first:
        dq_ref[...] = jnp.zeros_like(dq_ref)
    else:
        dq_ref[...] = state_refs[0][...]
    dk_ref[...] = jnp.zeros_like(dk_ref)
    dv_ref[...] = jnp.zeros_like(dv_ref)

    def body(b, j, q_rows, all_rows, hidden):
        every = [slice(h * HD, (h + 1) * HD) for h in range(heads)]
        query = [query_refs[b][q_rows, cols] for cols in every]
        dout = [dout_refs[b][q_rows, cols] for cols in every]
        lse = [stat_refs[b][h : h + 1, q_rows] for h in range(heads)]
        row_dot = [stat_refs[b][heads + h : heads + h + 1, q_rows] for h in range(heads)]
        key = [kv_refs[j][:, cols] for cols in every]
        value = [kv_refs[j][:, width + h * HD : width + (h + 1) * HD] for h in range(heads)]
        scores = [dot(key[h], query[h], NT) * SCALE2 for h in range(heads)]
        weights = [jnp.exp2(scores[h] - lse[h]) for h in range(heads)]
        if hidden is not None:
            weights = [jnp.where(hidden, 0.0, weight) for weight in weights]
        d_weights = [dot(value[h], dout[h], NT) for h in range(heads)]
        d_scores = [(weights[h] * (d_weights[h] - row_dot[h])).astype(BF16) for h in range(heads)]
        add_v = [dot(weights[h].astype(BF16), dout[h], NN) for h in range(heads)]
        add_k = [dot(d_scores[h], query[h], NN) for h in range(heads)]
        add_q = [dot(key[h], d_scores[h], TN) for h in range(heads)]
        for h, cols in enumerate(every):
            dv_ref[j, :, cols] += add_v[h]
            dk_ref[j, :, cols] += add_k[h]
            dq_ref[cols, all_rows] += add_q[h]

    pairs = [(j, b) for j in range(n_key) for b in range(2)]
    for_pairs(body, limit_ref, span_ref, base_ref, slab, pairs)
    for j in range(n_key):
        at = slice(j % 2 * slab, (j % 2 + 1) * slab)
        dkv_refs[j // 2][at, :width] = (dk_ref[j] * SCALE).astype(BF16)
        dkv_refs[j // 2][at, width:] = dv_ref[j].astype(BF16)
    if not last:
        return
    for b, out_ref in enumerate((own_ref, peer_ref)):
        for s in range(2):
            at = slice((2 * b + s) * slab, (2 * b + s + 1) * slab)
            for h in range(heads):
                cols = slice(h * HD, (h + 1) * HD)
                out_ref[s * slab : (s + 1) * slab, cols] = (dq_ref[cols, at] * SCALE).T.astype(out_ref.dtype)


def grad_kernel(steps, grad_hbm, w_hbm, out_ref, grad_ref, w_ref, grad_sem, w_sem):
    tile = grad_ref.shape[2]
    copies = []
    for k in range(steps):
        at = pl.ds(k * tile, tile)
        copies.append(
            (
                pltpu.make_async_copy(grad_hbm.at[:, at], grad_ref.at[k], grad_sem.at[k]),
                pltpu.make_async_copy(w_hbm.at[:, at], w_ref.at[k], w_sem.at[k]),
            )
        )
        for copy in copies[-1]:
            copy.start()
    total = None
    for k in range(steps):
        for copy in copies[k]:
            copy.wait()
        part = dot(grad_ref[k], w_ref[k], NT)
        total = part if total is None else total + part
    out_ref[...] = total.astype(BF16)


def project_grad(grad_rows, w_out, tile):
    rows, width, steps = grad_rows.shape[0], w_out.shape[0], w_out.shape[1] // tile
    hbm = pl.BlockSpec(memory_space=pltpu.MemorySpace.HBM)
    return pl.pallas_call(
        functools.partial(grad_kernel, steps),
        out_shape=jax.ShapeDtypeStruct((rows, width), BF16),
        in_specs=[hbm, hbm],
        out_specs=VMEM,
        scratch_shapes=[
            pltpu.VMEM((steps, rows, tile), BF16),
            pltpu.VMEM((steps, width, tile), BF16),
            pltpu.SemaphoreType.DMA((steps,)),
            pltpu.SemaphoreType.DMA((steps,)),
        ],
        compiler_params=pltpu.CompilerParams(vmem_limit_bytes=20 * 2**20),
        cost_estimate=CHEAP,
        name="project_grad",
    )(in_hbm(grad_rows), in_hbm(w_out))


def out_kernel(steps, at_ref, mixed_ref, other_ref, w_hbm, w_there_hbm, out_hbm, pair_ref, w_ref, out_ref, sems):
    width, tile = mixed_ref.shape[1], w_ref.shape[2]
    loads, stores = [], []
    for k in range(steps):
        cols = pl.ds(pl.multiple_of((at_ref[0] * steps + k) * tile, tile), tile)
        pair = [
            pltpu.make_async_copy(hbm.at[:, cols], w_ref.at[k, pl.ds(part * width, width), :], sems.at[part, k])
            for part, hbm in enumerate((w_hbm, w_there_hbm))
        ]
        for load in pair:
            load.start()
        loads.append(pair)
        stores.append(
            pltpu.make_async_copy(out_ref.at[k], out_hbm.at[:, pl.ds(k * tile, tile)], sems.at[2, k])
        )
    pair_ref[:, :width] = mixed_ref[...]
    pair_ref[:, width:] = other_ref[...]
    for k in range(steps):
        for load in loads[k]:
            load.wait()
        out_ref[k] = dot(pair_ref[...], w_ref[k], NN).astype(BF16)
        stores[k].start()
    for store in stores:
        store.wait()


def project_out(core, mixed, other, w_out, w_there, tile):
    (rows, width), half = mixed.shape, w_there.shape[1] // 2
    steps = half // tile
    hbm = pl.BlockSpec(memory_space=pltpu.MemorySpace.HBM)
    return pl.pallas_call(
        functools.partial(out_kernel, steps),
        out_shape=jax.ShapeDtypeStruct((rows, half), BF16),
        in_specs=[SMEM, VMEM, VMEM, hbm, hbm],
        out_specs=hbm,
        scratch_shapes=[
            pltpu.VMEM((rows, 2 * width), BF16),
            pltpu.VMEM((steps, 2 * width, tile), BF16),
            pltpu.VMEM((steps, rows, tile), BF16),
            pltpu.SemaphoreType.DMA((3, steps)),
        ],
        compiler_params=pltpu.CompilerParams(vmem_limit_bytes=20 * 2**20),
        cost_estimate=CHEAP,
        name="project_out",
    )(core.reshape(1).astype(jnp.int32), mixed, other, in_hbm(w_out), in_hbm(w_there))


CHEAP = pl.CostEstimate(flops=1, bytes_accessed=1, transcendentals=0)
SMEM = pl.BlockSpec(memory_space=pltpu.SMEM)
VMEM = pl.BlockSpec(memory_space=pltpu.VMEM)
LIMIT = 16 * 2**20


def add_kernel(a_ref, b_ref, out_ref):
    out_ref[...] = (a_ref[...].astype(F32) + b_ref[...].astype(F32)).astype(out_ref.dtype)


def kv_kernel(early_ref, next_ref, prev_ref, k_ref, v_ref):
    width = k_ref.shape[1]
    for out_ref, cols in ((k_ref, slice(0, width)), (v_ref, slice(width, 2 * width))):
        total = early_ref[:, cols] + next_ref[:, cols].astype(F32) + prev_ref[:, cols].astype(F32)
        out_ref[...] = total.astype(BF16)


def part_kernel(at_ref, rows_ref, out_ref):
    few = out_ref.shape[0]
    out_ref[...] = rows_ref[pl.ds(pl.multiple_of(at_ref[0] * few, few), few), :]


def out_sum_kernel(at_ref, rows_ref, from_ref, here_ref, there_ref):
    few = here_ref.shape[0]
    for out_ref, core in ((here_ref, at_ref[1]), (there_ref, 1 - at_ref[1])):
        mine = rows_ref[pl.ds(pl.multiple_of((at_ref[0] * 2 + core) * few, few), few), :]
        other = from_ref[pl.ds(pl.multiple_of(core * few, few), few), :]
        out_ref[...] = (mine.astype(F32) + other.astype(F32)).astype(BF16)


def call(kernel, outs, n_scalar, n_vector, scratch, name, flops=1):
    return pl.pallas_call(
        kernel,
        out_shape=[jax.ShapeDtypeStruct(shape, dtype) for shape, dtype in outs],
        in_specs=[SMEM] * n_scalar + [VMEM] * n_vector,
        out_specs=[VMEM] * len(outs),
        scratch_shapes=scratch,
        compiler_params=pltpu.CompilerParams(vmem_limit_bytes=LIMIT),
        cost_estimate=pl.CostEstimate(flops=flops, bytes_accessed=1, transcendentals=0),
        name=name,
    )


def on_device(queries, keys, values, w_out, grad_out, slab_order, frame_lengths):
    rows, width = queries.shape
    heads, slab = width // HD, rows // 2
    n_head = lax.axis_size("head")
    half = w_out.shape[1] // 2
    ctx, head = lax.axis_index("ctx"), lax.axis_index("head")
    core = head % 2

    def over_x(array, o):
        perm = [(y * 4 + x, y * 4 + (x - o) % 4) for y in range(2) for x in range(4)]
        return lax.ppermute(array, "ctx", perm)

    def over_y(array):
        return lax.ppermute(array, "ctx", [(c, (c + 4) % 8) for c in range(8)])

    def over_core(array):
        return lax.ppermute(array, "head", [(h, h ^ 1) for h in range(n_head)])

    def over_chips(array, dz, dy):
        perm = [(h, ((h // 4 + dz) % 4) * 4 + (h ^ (2 * dy)) % 4) for h in range(n_head)]
        return lax.ppermute(array, "head", perm)

    offsets = (0, 1, 3, 2)
    base = ctx // 4 * 4
    slots = [(base + (ctx + o) % 4) * 2 + s for o in offsets for s in range(2)]
    places = jnp.stack([ctx, (ctx + 4) % 8] + slots).astype(jnp.int32)
    facts = jnp.concatenate([places, slab_order, frame_lengths])
    part = (rows, width)
    stat = (8, rows)

    def masks(n_key):
        return [
            pltpu.VMEM((1, 2 * rows), jnp.int32),
            pltpu.SMEM((4, 2), jnp.int32),
            pltpu.SMEM((n_key,), jnp.int32),
        ]

    def forward(keys, pairs, state, last):
        n_key, n_query = len(keys), 1 + max(b for _, b in pairs)
        states = [((width, 2 * rows), F32), ((8, 2 * rows), F32), ((8, 2 * rows), F32)]
        results = [(part, F32), (stat, F32), (part, BF16), (stat, F32)]
        return call(
            functools.partial(forward_kernel, keys, pairs, heads, slab, not state, last),
            results if last else states,
            1,
            n_query + n_key + len(state),
            [pltpu.VMEM(*s) for s in states if last] + masks(n_key),
            "forward",
        )(facts, *(queries, peer_queries)[:n_query], *(kv[k] for k in keys), *state)

    def backward(keys, state, last):
        n_key, n_block = len(keys), len(keys) // 2
        states = [((width, 2 * rows), F32)]
        results = [(part, F32), (part, BF16)]
        scratch = [
            pltpu.VMEM((n_key, slab, width), F32),
            pltpu.VMEM((n_key, slab, width), F32),
        ]
        outs = call(
            functools.partial(backward_kernel, keys, heads, slab, not state, last),
            [((rows, 2 * width), BF16)] * n_block + (results if last else states),
            1,
            6 + n_key + len(state),
            [pltpu.VMEM(*s) for s in states if last] + scratch + masks(n_key),
            "backward",
        )(
            facts,
            queries,
            peer_queries,
            grad_mixed,
            peer_grad,
            stats,
            peer_stats,
            *(kv[k] for k in keys),
            *state,
        )
        return outs[:n_block], outs[n_block:]

    peer_queries = over_y(queries)
    kv = [jnp.concatenate([keys[at], values[at]], axis=1) for at in (slice(0, slab), slice(slab, rows))]
    next_0, prev_1 = over_x(kv[0], 1), over_x(kv[1], 3)
    next_1, prev_0 = over_x(kv[1], 1), over_x(kv[0], 3)
    grad_rows = lax.all_gather(grad_out, "head", axis=0, tiled=True)
    w_there = over_core(w_out)
    state = forward((0, 1), ((0, 0), (1, 0)), [], False)
    next_0, prev_1, *state = lax.optimization_barrier((next_0, prev_1, *state))
    kv += [next_0, next_1, prev_0, prev_1, over_x(next_0, 1), over_x(prev_1, 3)]
    w_there, *state = lax.optimization_barrier((w_there, *state))
    state = forward((0, 1, 2, 5), ((0, 1), (1, 1), (2, 0), (2, 1), (3, 0), (3, 1)), state, False)
    every = tuple((j, b) for j in range(4) for b in range(2))
    own_mixed, own_lse, peer_mixed, peer_lse = forward((3, 4, 6, 7), every, state, True)
    from_lse, from_mixed = over_y(peer_lse), over_y(peer_mixed)

    grad_rows, peer_lse = lax.optimization_barrier((grad_rows, peer_lse))
    grad_mixed = project_grad(grad_rows, w_out, 1024)
    peer_grad = over_y(grad_mixed)
    from_mixed, grad_mixed = lax.optimization_barrier((from_mixed, grad_mixed))

    mixed, lse = call(
        functools.partial(merge_kernel, heads, slab),
        [(part, BF16), (stat, F32)],
        0,
        4,
        [],
        "merge",
    )(own_mixed, own_lse, from_mixed, from_lse)
    (stats,) = call(
        functools.partial(stats_kernel, heads, slab), [(stat, F32)], 0, 3, [], "stats"
    )(mixed, grad_mixed, lse)
    peer_stats = over_y(stats)

    out_part = project_out(core, mixed, over_core(mixed), w_out, w_there, 512)
    z_groups = [[z * 4 + r for z in range(4)] for r in range(4)]
    out_part, peer_grad, peer_stats = lax.optimization_barrier((out_part, peer_grad, peer_stats))
    out_rows = lax.psum_scatter(
        out_part, "head", scatter_dimension=0, tiled=True, axis_index_groups=z_groups
    )

    (far_dkv,), state = backward((6, 7), [], False)
    far_dkv = over_x(far_dkv, 2)
    (next_dkv, prev_dkv), state = backward((2, 3, 4, 5), state, False)
    next_dkv, prev_dkv = over_x(next_dkv, 3), over_x(prev_dkv, 1)
    (own_dkv,), (own_dq, peer_dq) = backward((0, 1), state, True)
    peer_dq = over_y(peer_dq)

    own_dkv, far_dkv = lax.optimization_barrier((own_dkv, far_dkv))
    short = 3 * 10**8
    (kv_early,) = call(add_kernel, [((rows, 2 * width), F32)], 0, 2, [], "kv_early", short)(own_dkv, far_dkv)
    kv_early, next_dkv, prev_dkv = lax.optimization_barrier((kv_early, next_dkv, prev_dkv))
    k_grad, v_grad = call(kv_kernel, [(part, BF16)] * 2, 0, 3, [], "kv_sum")(kv_early, next_dkv, prev_dkv)
    own_dq, peer_dq, k_grad = lax.optimization_barrier((own_dq, peer_dq, k_grad))
    (q_grad,) = call(add_kernel, [(part, BF16)], 0, 2, [], "q_sum", short)(own_dq, peer_dq)

    few = 2 * rows // n_head // 2
    y_lo = head // 2 % 2
    spot = jnp.stack([y_lo, core]).astype(jnp.int32)
    (to_send,) = call(part_kernel, [((2 * few, half), BF16)], 1, 1, [], "out_piece")(1 - spot, out_rows)
    received = over_chips(to_send, 0, 1)
    received, k_grad, q_grad = lax.optimization_barrier((received, k_grad, q_grad))
    here, there = call(out_sum_kernel, [((few, half), BF16)] * 2, 1, 2, [], "out_sum")(spot, out_rows, received)
    there = over_core(there)
    layer_out = jnp.concatenate(
        [jnp.where(core == 0, here, there), jnp.where(core == 0, there, here)], axis=1
    )
    return layer_out, q_grad, k_grad, v_grad


def solution(mesh):
    in_specs = (
        P("ctx", "head"),
        P("ctx", "head"),
        P("ctx", "head"),
        P("head", None),
        P(("ctx", "head"), None),
        P(),
        P(),
    )
    out_specs = (P(("ctx", "head"), None), P("ctx", "head"), P("ctx", "head"), P("ctx", "head"))
    return jax.shard_map(on_device, mesh=mesh, in_specs=in_specs, out_specs=out_specs, check_vma=False)
```

```python
import functools
import math

import jax
import jax.numpy as jnp
from jax import lax
from jax.experimental import pallas as pl
from jax.experimental.pallas import tpu as pltpu
from jax.sharding import PartitionSpec as P

HD = 128
LOG2E = math.log2(math.e)
SCALE = float(HD) ** -0.5
SCALE2 = SCALE * LOG2E
START_MAX = -1e20
HIDDEN = -1e30
F32, BF16 = jnp.float32, jnp.bfloat16
NT = (((1,), (1,)), ((), ()))
TN = (((0,), (0,)), ((), ()))
NN = (((1,), (0,)), ((), ()))


def in_hbm(array):
    return pltpu.with_memory_space_constraint(array, pltpu.MemorySpace.HBM)


def dot(a, b, dims):
    return lax.dot_general(a, b, dims, preferred_element_type=F32)


def last_visible(ends, pos):
    limit = ends[-1]
    for end in reversed(ends[:-1]):
        limit = jnp.where(end > pos, end, limit)
    return limit


def visibility(facts_ref, limit_ref, span_ref, base_ref, slab, keys):
    n_slot = 8
    order, length = 2 + n_slot, 2 + n_slot + (facts_ref.shape[0] - 2 - n_slot) // 2
    ends, total = [], jnp.int32(0)
    for f in range(length, facts_ref.shape[0]):
        total = total + facts_ref[f]
        ends.append(total)
    for i in range(4):
        base = facts_ref[order + facts_ref[i // 2] * 2 + i % 2] * slab
        rows = base + lax.broadcasted_iota(jnp.int32, (1, slab), 1)
        limit_ref[:, i * slab : (i + 1) * slab] = last_visible(ends, rows)
        span_ref[i, 0] = last_visible(ends, base)
        span_ref[i, 1] = last_visible(ends, base + slab - 1)
    for j, key in enumerate(keys):
        base_ref[j] = facts_ref[order + facts_ref[2 + key]] * slab


def for_pairs(body, limit_ref, span_ref, base_ref, slab, pairs):
    for j, b in pairs:

        def step(i, carry, b=b, j=j):
            base = base_ref[j]
            low, high = span_ref[2 * b + i, 0], span_ref[2 * b + i, 1]
            q_rows = pl.ds(pl.multiple_of(i * slab, slab), slab)
            all_rows = pl.ds(pl.multiple_of((2 * b + i) * slab, slab), slab)

            @pl.when(base + slab <= low)
            def _():
                body(b, j, q_rows, all_rows, None)

            @pl.when(jnp.logical_and(base < high, base + slab > low))
            def _():
                limit = limit_ref[:, all_rows] - base
                hidden = lax.broadcasted_iota(jnp.int32, (slab, slab), 0) >= limit
                body(b, j, q_rows, all_rows, hidden)

            return carry

        lax.fori_loop(0, 2, step, 0)


def forward_kernel(keys, pairs, heads, slab, first, last, *refs):
    facts_ref, *refs = refs
    n_key = len(keys)
    n_query = 1 + max(b for _, b in pairs)
    query_refs, refs = refs[:n_query], refs[n_query:]
    kv_refs, refs = refs[:n_key], refs[n_key:]
    state_refs, refs = ([], refs) if first else (refs[:3], refs[3:])
    if last:
        own_ref, own_lse_ref, peer_ref, peer_lse_ref, *refs = refs
    acc_ref, max_ref, sum_ref, limit_ref, span_ref, base_ref = refs
    rows, width = 2 * slab, heads * HD
    visibility(facts_ref, limit_ref, span_ref, base_ref, slab, keys)
    if first:
        acc_ref[...] = jnp.zeros_like(acc_ref)
        max_ref[...] = jnp.full_like(max_ref, START_MAX)
        sum_ref[...] = jnp.zeros_like(sum_ref)
    else:
        for to_ref, from_ref in zip((acc_ref, max_ref, sum_ref), state_refs):
            to_ref[...] = from_ref[...]

    def body(b, j, q_rows, all_rows, hidden):
        every = [slice(h * HD, (h + 1) * HD) for h in range(heads)]
        key = [kv_refs[j][:, cols] for cols in every]
        value = [kv_refs[j][:, width + h * HD : width + (h + 1) * HD] for h in range(heads)]
        old = [max_ref[h : h + 1, all_rows] for h in range(heads)]
        scores = [dot(key[h], query_refs[b][q_rows, cols], NT) * SCALE2 for h, cols in enumerate(every)]
        if hidden is not None:
            scores = [jnp.where(hidden, HIDDEN, score) for score in scores]
        new = [jnp.maximum(m, jnp.max(x, axis=0, keepdims=True)) for m, x in zip(old, scores)]
        weights = [jnp.exp2(x - m) for x, m in zip(scores, new)]
        fades = [jnp.exp2(m - n) for m, n in zip(old, new)]
        sums = [
            sum_ref[h : h + 1, all_rows] * fades[h] + jnp.sum(weights[h], axis=0, keepdims=True)
            for h in range(heads)
        ]
        mixes = [dot(v, w.astype(BF16), TN) for v, w in zip(value, weights)]
        for h, cols in enumerate(every):
            max_ref[h : h + 1, all_rows] = new[h]
            sum_ref[h : h + 1, all_rows] = sums[h]
            acc_ref[cols, all_rows] = acc_ref[cols, all_rows] * fades[h] + mixes[h]

    for_pairs(body, limit_ref, span_ref, base_ref, slab, pairs)
    if not last:
        return
    total = jnp.maximum(sum_ref[...], 1e-30)
    lse = max_ref[...] + jnp.log2(total)
    own_lse_ref[...] = lse[:, :rows]
    peer_lse_ref[...] = lse[:, rows:]
    for b, out_ref in enumerate((own_ref, peer_ref)):
        for s in range(2):
            at = slice((2 * b + s) * slab, (2 * b + s + 1) * slab)
            for h in range(heads):
                cols = slice(h * HD, (h + 1) * HD)
                mixed = acc_ref[cols, at] / total[h : h + 1, at]
                out_ref[s * slab : (s + 1) * slab, cols] = mixed.T.astype(out_ref.dtype)


def merge_kernel(heads, slab, own_ref, own_lse_ref, from_ref, from_lse_ref, dout_ref, mixed_ref, stats_ref):
    a, b = own_lse_ref[...], from_lse_ref[...]
    top = jnp.maximum(a, b)
    lse = top + jnp.log2(jnp.exp2(a - top) + jnp.exp2(b - top))
    stats_ref[...] = lse
    share_a, share_b = jnp.exp2(a - lse), jnp.exp2(b - lse)
    for s in range(2):
        at = slice(s * slab, (s + 1) * slab)
        for h in range(heads):
            cols = slice(h * HD, (h + 1) * HD)
            wa = jnp.broadcast_to(share_a[h : h + 1, at], (HD, slab)).T
            wb = jnp.broadcast_to(share_b[h : h + 1, at], (HD, slab)).T
            mixed = (own_ref[at, cols] * wa + from_ref[at, cols].astype(F32) * wb).astype(BF16)
            mixed_ref[at, cols] = mixed
            prod = mixed.astype(F32) * dout_ref[at, cols].astype(F32)
            stats_ref[heads + h : heads + h + 1, at] = jnp.sum(prod.T, axis=0, keepdims=True)


def backward_kernel(keys, heads, slab, first, last, *refs):
    facts_ref, *refs = refs
    n_key = len(keys)
    query_refs, dout_refs, stat_refs, refs = refs[:2], refs[2:4], refs[4:6], refs[6:]
    kv_refs, refs = refs[:n_key], refs[n_key:]
    state_refs, refs = ([], refs) if first else (refs[:1], refs[1:])
    dkv_refs, refs = refs[: n_key // 2], refs[n_key // 2 :]
    if last:
        own_ref, peer_ref, *refs = refs
    dq_ref, dk_ref, dv_ref, limit_ref, span_ref, base_ref = refs
    rows, width = 2 * slab, heads * HD
    visibility(facts_ref, limit_ref, span_ref, base_ref, slab, keys)
    if first:
        dq_ref[...] = jnp.zeros_like(dq_ref)
    else:
        dq_ref[...] = state_refs[0][...]
    dk_ref[...] = jnp.zeros_like(dk_ref)
    dv_ref[...] = jnp.zeros_like(dv_ref)

    def body(b, j, q_rows, all_rows, hidden):
        every = [slice(h * HD, (h + 1) * HD) for h in range(heads)]
        query = [query_refs[b][q_rows, cols] for cols in every]
        dout = [dout_refs[b][q_rows, cols] for cols in every]
        lse = [stat_refs[b][h : h + 1, q_rows] for h in range(heads)]
        row_dot = [stat_refs[b][heads + h : heads + h + 1, q_rows] for h in range(heads)]
        key = [kv_refs[j][:, cols] for cols in every]
        value = [kv_refs[j][:, width + h * HD : width + (h + 1) * HD] for h in range(heads)]
        scores = [dot(key[h], query[h], NT) * SCALE2 for h in range(heads)]
        weights = [jnp.exp2(scores[h] - lse[h]) for h in range(heads)]
        if hidden is not None:
            weights = [jnp.where(hidden, 0.0, weight) for weight in weights]
        d_weights = [dot(value[h], dout[h], NT) for h in range(heads)]
        d_scores = [(weights[h] * (d_weights[h] - row_dot[h])).astype(BF16) for h in range(heads)]
        add_v = [dot(weights[h].astype(BF16), dout[h], NN) for h in range(heads)]
        add_k = [dot(d_scores[h], query[h], NN) for h in range(heads)]
        add_q = [dot(key[h], d_scores[h], TN) for h in range(heads)]
        for h, cols in enumerate(every):
            dv_ref[j, :, cols] += add_v[h]
            dk_ref[j, :, cols] += add_k[h]
            dq_ref[cols, all_rows] += add_q[h]

    pairs = [(j, b) for j in range(n_key) for b in range(2)]
    for_pairs(body, limit_ref, span_ref, base_ref, slab, pairs)
    for j in range(n_key):
        at = slice(j % 2 * slab, (j % 2 + 1) * slab)
        dkv_refs[j // 2][at, :width] = (dk_ref[j] * SCALE).astype(BF16)
        dkv_refs[j // 2][at, width:] = dv_ref[j].astype(BF16)
    if not last:
        return
    for b, out_ref in enumerate((own_ref, peer_ref)):
        for s in range(2):
            at = slice((2 * b + s) * slab, (2 * b + s + 1) * slab)
            for h in range(heads):
                cols = slice(h * HD, (h + 1) * HD)
                out_ref[s * slab : (s + 1) * slab, cols] = (dq_ref[cols, at] * SCALE).T.astype(out_ref.dtype)


def grad_kernel(steps, grad_hbm, w_hbm, out_ref, grad_ref, w_ref, grad_sem, w_sem):
    tile = grad_ref.shape[2]
    copies = []
    for k in range(steps):
        at = pl.ds(k * tile, tile)
        copies.append(
            (
                pltpu.make_async_copy(grad_hbm.at[:, at], grad_ref.at[k], grad_sem.at[k]),
                pltpu.make_async_copy(w_hbm.at[:, at], w_ref.at[k], w_sem.at[k]),
            )
        )
        for copy in copies[-1]:
            copy.start()
    total = None
    for k in range(steps):
        for copy in copies[k]:
            copy.wait()
        part = dot(grad_ref[k], w_ref[k], NT)
        total = part if total is None else total + part
    out_ref[...] = total.astype(BF16)


def project_grad(grad_rows, w_out, tile):
    rows, width, steps = grad_rows.shape[0], w_out.shape[0], w_out.shape[1] // tile
    hbm = pl.BlockSpec(memory_space=pltpu.MemorySpace.HBM)
    return pl.pallas_call(
        functools.partial(grad_kernel, steps),
        out_shape=jax.ShapeDtypeStruct((rows, width), BF16),
        in_specs=[hbm, hbm],
        out_specs=VMEM,
        scratch_shapes=[
            pltpu.VMEM((steps, rows, tile), BF16),
            pltpu.VMEM((steps, width, tile), BF16),
            pltpu.SemaphoreType.DMA((steps,)),
            pltpu.SemaphoreType.DMA((steps,)),
        ],
        compiler_params=pltpu.CompilerParams(vmem_limit_bytes=20 * 2**20),
        cost_estimate=CHEAP,
        name="project_grad",
    )(in_hbm(grad_rows), in_hbm(w_out))


def out_kernel(steps, at_ref, mixed_ref, other_ref, w_hbm, w_there_hbm, out_hbm, pair_ref, w_ref, out_ref, sems):
    width, tile = mixed_ref.shape[1], w_ref.shape[2]
    loads, stores = [], []
    for k in range(steps):
        cols = pl.ds(pl.multiple_of((at_ref[0] * steps + k) * tile, tile), tile)
        pair = [
            pltpu.make_async_copy(hbm.at[:, cols], w_ref.at[k, pl.ds(part * width, width), :], sems.at[part, k])
            for part, hbm in enumerate((w_hbm, w_there_hbm))
        ]
        for load in pair:
            load.start()
        loads.append(pair)
        stores.append(
            pltpu.make_async_copy(out_ref.at[k], out_hbm.at[:, pl.ds(k * tile, tile)], sems.at[2, k])
        )
    pair_ref[:, :width] = mixed_ref[...]
    pair_ref[:, width:] = other_ref[...]
    for k in range(steps):
        for load in loads[k]:
            load.wait()
        out_ref[k] = dot(pair_ref[...], w_ref[k], NN).astype(BF16)
        stores[k].start()
    for store in stores:
        store.wait()


def project_out(core, mixed, other, w_out, w_there, tile):
    (rows, width), half = mixed.shape, w_there.shape[1] // 2
    steps = half // tile
    hbm = pl.BlockSpec(memory_space=pltpu.MemorySpace.HBM)
    return pl.pallas_call(
        functools.partial(out_kernel, steps),
        out_shape=pltpu.MemorySpace.HBM((rows, half), BF16),
        in_specs=[SMEM, VMEM, VMEM, hbm, hbm],
        out_specs=hbm,
        scratch_shapes=[
            pltpu.VMEM((rows, 2 * width), BF16),
            pltpu.VMEM((steps, 2 * width, tile), BF16),
            pltpu.VMEM((steps, rows, tile), BF16),
            pltpu.SemaphoreType.DMA((3, steps)),
        ],
        compiler_params=pltpu.CompilerParams(vmem_limit_bytes=20 * 2**20),
        cost_estimate=CHEAP,
        name="project_out",
    )(core.reshape(1).astype(jnp.int32), mixed, other, in_hbm(w_out), in_hbm(w_there))


CHEAP = pl.CostEstimate(flops=1, bytes_accessed=1, transcendentals=0)
SMEM = pl.BlockSpec(memory_space=pltpu.SMEM)
VMEM = pl.BlockSpec(memory_space=pltpu.VMEM)
LIMIT = 16 * 2**20


def add_kernel(a_ref, b_ref, out_ref):
    out_ref[...] = (a_ref[...].astype(F32) + b_ref[...].astype(F32)).astype(out_ref.dtype)


def kv_kernel(early_ref, next_ref, prev_ref, k_ref, v_ref):
    width = k_ref.shape[1]
    for out_ref, cols in ((k_ref, slice(0, width)), (v_ref, slice(width, 2 * width))):
        total = early_ref[:, cols] + next_ref[:, cols].astype(F32) + prev_ref[:, cols].astype(F32)
        out_ref[...] = total.astype(BF16)


def part_kernel(at_ref, rows_ref, out_ref):
    few = out_ref.shape[0]
    out_ref[...] = rows_ref[pl.ds(pl.multiple_of(at_ref[0] * few, few), few), :]


def out_sum_kernel(at_ref, rows_ref, from_ref, here_ref, there_ref):
    few = here_ref.shape[0]
    for out_ref, core in ((here_ref, at_ref[1]), (there_ref, 1 - at_ref[1])):
        mine = rows_ref[pl.ds(pl.multiple_of((at_ref[0] * 2 + core) * few, few), few), :]
        other = from_ref[pl.ds(pl.multiple_of(core * few, few), few), :]
        out_ref[...] = (mine.astype(F32) + other.astype(F32)).astype(BF16)


def call(kernel, outs, n_scalar, n_vector, scratch, name, flops=1):
    return pl.pallas_call(
        kernel,
        out_shape=[jax.ShapeDtypeStruct(shape, dtype) for shape, dtype in outs],
        in_specs=[SMEM] * n_scalar + [VMEM] * n_vector,
        out_specs=[VMEM] * len(outs),
        scratch_shapes=scratch,
        compiler_params=pltpu.CompilerParams(vmem_limit_bytes=LIMIT),
        cost_estimate=pl.CostEstimate(flops=flops, bytes_accessed=1, transcendentals=0),
        name=name,
    )


def on_device(queries, keys, values, w_out, grad_out, slab_order, frame_lengths):
    rows, width = queries.shape
    heads, slab = width // HD, rows // 2
    n_head = lax.axis_size("head")
    half = w_out.shape[1] // 2
    ctx, head = lax.axis_index("ctx"), lax.axis_index("head")
    core = head % 2

    def over_x(array, o):
        perm = [(y * 4 + x, y * 4 + (x - o) % 4) for y in range(2) for x in range(4)]
        return lax.ppermute(array, "ctx", perm)

    def over_y(array):
        return lax.ppermute(array, "ctx", [(c, (c + 4) % 8) for c in range(8)])

    def over_core(array):
        return lax.ppermute(array, "head", [(h, h ^ 1) for h in range(n_head)])

    def over_chips(array, dz, dy):
        perm = [(h, ((h // 4 + dz) % 4) * 4 + (h ^ (2 * dy)) % 4) for h in range(n_head)]
        return lax.ppermute(array, "head", perm)

    offsets = (0, 1, 3, 2)
    base = ctx // 4 * 4
    slots = [(base + (ctx + o) % 4) * 2 + s for o in offsets for s in range(2)]
    places = jnp.stack([ctx, (ctx + 4) % 8] + slots).astype(jnp.int32)
    facts = jnp.concatenate([places, slab_order, frame_lengths])
    part = (rows, width)
    stat = (8, rows)

    def masks(n_key):
        return [
            pltpu.VMEM((1, 2 * rows), jnp.int32),
            pltpu.SMEM((4, 2), jnp.int32),
            pltpu.SMEM((n_key,), jnp.int32),
        ]

    def forward(keys, pairs, state, last):
        n_key, n_query = len(keys), 1 + max(b for _, b in pairs)
        states = [((width, 2 * rows), F32), ((8, 2 * rows), F32), ((8, 2 * rows), F32)]
        results = [(part, F32), (stat, F32), (part, BF16), (stat, F32)]
        return call(
            functools.partial(forward_kernel, keys, pairs, heads, slab, not state, last),
            results if last else states,
            1,
            n_query + n_key + len(state),
            [pltpu.VMEM(*s) for s in states if last] + masks(n_key),
            "forward",
        )(facts, *(queries, peer_queries)[:n_query], *(in_hbm(kv[k]) for k in keys), *state)

    def backward(keys, state, last):
        n_key, n_block = len(keys), len(keys) // 2
        states = [((width, 2 * rows), F32)]
        results = [(part, F32), (part, BF16)]
        scratch = [
            pltpu.VMEM((n_key, slab, width), F32),
            pltpu.VMEM((n_key, slab, width), F32),
        ]
        outs = call(
            functools.partial(backward_kernel, keys, heads, slab, not state, last),
            [((rows, 2 * width), BF16)] * n_block + (results if last else states),
            1,
            6 + n_key + len(state),
            [pltpu.VMEM(*s) for s in states if last] + scratch + masks(n_key),
            "backward",
        )(
            facts,
            queries,
            peer_queries,
            grad_mixed,
            peer_grad,
            stats,
            peer_stats,
            *(in_hbm(kv[k]) for k in keys),
            *(in_hbm(array) for array in state),
        )
        return outs[:n_block], outs[n_block:]

    peer_queries = over_y(queries)
    kv = [jnp.concatenate([keys[at], values[at]], axis=1) for at in (slice(0, slab), slice(slab, rows))]
    next_0, prev_1 = over_x(kv[0], 1), over_x(kv[1], 3)
    next_1, prev_0 = over_x(kv[1], 1), over_x(kv[0], 3)
    grad_rows = lax.all_gather(grad_out, "head", axis=0, tiled=True)
    w_there = over_core(w_out)
    state = forward((0, 1), ((0, 0), (1, 0)), [], False)
    next_0, prev_1, *state = lax.optimization_barrier((next_0, prev_1, *state))
    kv += [next_0, next_1, prev_0, prev_1, over_x(next_0, 1), over_x(prev_1, 3)]
    w_there, *state = lax.optimization_barrier((w_there, *state))
    state = forward((0, 1, 2, 5), ((0, 1), (1, 1), (2, 0), (2, 1), (3, 0), (3, 1)), state, False)
    every = tuple((j, b) for j in range(2) for b in range(2))
    state = forward((3, 4), every, state, False)
    own_mixed, own_lse, peer_mixed, peer_lse = forward((6, 7), every, state, True)
    from_lse, from_mixed = over_y(peer_lse), over_y(peer_mixed)

    grad_rows, peer_lse = lax.optimization_barrier((grad_rows, peer_lse))
    grad_mixed = project_grad(grad_rows, w_out, 1024)
    peer_grad = over_y(grad_mixed)
    mixed, stats = call(
        functools.partial(merge_kernel, heads, slab),
        [(part, BF16), (stat, F32)],
        0,
        5,
        [],
        "merge",
    )(in_hbm(own_mixed), in_hbm(own_lse), from_mixed, in_hbm(from_lse), grad_mixed)
    peer_stats = over_y(stats)

    out_part = project_out(core, mixed, over_core(mixed), w_out, w_there, 512)
    z_groups = [[z * 4 + r for z in range(4)] for r in range(4)]
    out_part, peer_grad, peer_stats = lax.optimization_barrier((out_part, peer_grad, peer_stats))
    out_rows = lax.psum_scatter(
        out_part, "head", scatter_dimension=0, tiled=True, axis_index_groups=z_groups
    )

    (far_dkv,), state = backward((6, 7), [], False)
    far_dkv = over_x(far_dkv, 2)
    (next_dkv, prev_dkv), state = backward((2, 3, 4, 5), state, False)
    next_dkv, prev_dkv = over_x(next_dkv, 3), over_x(prev_dkv, 1)
    (own_dkv,), (own_dq, peer_dq) = backward((0, 1), state, True)
    peer_dq = over_y(peer_dq)

    own_dkv, far_dkv = lax.optimization_barrier((own_dkv, far_dkv))
    short = 3 * 10**8
    (kv_early,) = call(add_kernel, [((rows, 2 * width), F32)], 0, 2, [], "kv_early", short)(
        in_hbm(own_dkv), far_dkv
    )
    kv_early, next_dkv, prev_dkv = lax.optimization_barrier((kv_early, next_dkv, prev_dkv))
    k_grad, v_grad = call(kv_kernel, [(part, BF16)] * 2, 0, 3, [], "kv_sum")(kv_early, next_dkv, prev_dkv)
    own_dq, peer_dq, k_grad = lax.optimization_barrier((own_dq, peer_dq, k_grad))
    (q_grad,) = call(add_kernel, [(part, BF16)], 0, 2, [], "q_sum", short)(own_dq, peer_dq)

    few = 2 * rows // n_head // 2
    y_lo = head // 2 % 2
    spot = jnp.stack([y_lo, core]).astype(jnp.int32)
    (to_send,) = call(part_kernel, [((2 * few, half), BF16)], 1, 1, [], "out_piece")(1 - spot, in_hbm(out_rows))
    received = over_chips(to_send, 0, 1)
    received, k_grad, q_grad = lax.optimization_barrier((received, k_grad, q_grad))
    here, there = call(out_sum_kernel, [((few, half), BF16)] * 2, 1, 2, [], "out_sum")(spot, in_hbm(out_rows), received)
    there = over_core(there)
    layer_out = jnp.concatenate(
        [jnp.where(core == 0, here, there), jnp.where(core == 0, there, here)], axis=1
    )
    return layer_out, q_grad, k_grad, v_grad


def solution(mesh):
    in_specs = (
        P("ctx", "head"),
        P("ctx", "head"),
        P("ctx", "head"),
        P("head", None),
        P(("ctx", "head"), None),
        P(),
        P(),
    )
    out_specs = (P(("ctx", "head"), None), P("ctx", "head"), P("ctx", "head"), P("ctx", "head"))
    return jax.shard_map(on_device, mesh=mesh, in_specs=in_specs, out_specs=out_specs, check_vma=False)
```

```python
import functools
import math

import jax
import jax.numpy as jnp
from jax import lax
from jax.experimental import pallas as pl
from jax.experimental.pallas import tpu as pltpu
from jax.sharding import PartitionSpec as P

HD = 128
LOG2E = math.log2(math.e)
SCALE = float(HD) ** -0.5
SCALE2 = SCALE * LOG2E
START_MAX = -1e20
HIDDEN = -1e30
F32, BF16 = jnp.float32, jnp.bfloat16
NT = (((1,), (1,)), ((), ()))
TN = (((0,), (0,)), ((), ()))
NN = (((1,), (0,)), ((), ()))


def in_hbm(array):
    return pltpu.with_memory_space_constraint(array, pltpu.MemorySpace.HBM)


def dot(a, b, dims):
    return lax.dot_general(a, b, dims, preferred_element_type=F32)


def last_visible(ends, pos):
    limit = ends[-1]
    for end in reversed(ends[:-1]):
        limit = jnp.where(end > pos, end, limit)
    return limit


def visibility(facts_ref, limit_ref, span_ref, base_ref, slab, keys):
    n_slot = 8
    order, length = 2 + n_slot, 2 + n_slot + (facts_ref.shape[0] - 2 - n_slot) // 2
    ends, total = [], jnp.int32(0)
    for f in range(length, facts_ref.shape[0]):
        total = total + facts_ref[f]
        ends.append(total)
    for i in range(4):
        base = facts_ref[order + facts_ref[i // 2] * 2 + i % 2] * slab
        rows = base + lax.broadcasted_iota(jnp.int32, (1, slab), 1)
        limit_ref[:, i * slab : (i + 1) * slab] = last_visible(ends, rows)
        span_ref[i, 0] = last_visible(ends, base)
        span_ref[i, 1] = last_visible(ends, base + slab - 1)
    for j, key in enumerate(keys):
        base_ref[j] = facts_ref[order + facts_ref[2 + key]] * slab


def for_pairs(body, limit_ref, span_ref, base_ref, slab, pairs):
    for j, b in pairs:

        def step(i, carry, b=b, j=j):
            base = base_ref[j]
            low, high = span_ref[2 * b + i, 0], span_ref[2 * b + i, 1]
            q_rows = pl.ds(pl.multiple_of(i * slab, slab), slab)
            all_rows = pl.ds(pl.multiple_of((2 * b + i) * slab, slab), slab)

            @pl.when(base + slab <= low)
            def _():
                body(b, j, q_rows, all_rows, None)

            @pl.when(jnp.logical_and(base < high, base + slab > low))
            def _():
                limit = limit_ref[:, all_rows] - base
                hidden = lax.broadcasted_iota(jnp.int32, (slab, slab), 0) >= limit
                body(b, j, q_rows, all_rows, hidden)

            return carry

        lax.fori_loop(0, 2, step, 0)


def forward_kernel(keys, pairs, heads, slab, first, last, *refs):
    facts_ref, *refs = refs
    n_key = len(keys)
    n_query = 1 + max(b for _, b in pairs)
    query_refs, refs = refs[:n_query], refs[n_query:]
    kv_refs, refs = refs[:n_key], refs[n_key:]
    state_refs, refs = ([], refs) if first else (refs[:3], refs[3:])
    if last:
        own_ref, own_lse_ref, peer_ref, peer_lse_ref, *refs = refs
    acc_ref, max_ref, sum_ref, limit_ref, span_ref, base_ref = refs
    rows, width = 2 * slab, heads * HD
    visibility(facts_ref, limit_ref, span_ref, base_ref, slab, keys)
    if first:
        acc_ref[...] = jnp.zeros_like(acc_ref)
        max_ref[...] = jnp.full_like(max_ref, START_MAX)
        sum_ref[...] = jnp.zeros_like(sum_ref)
    else:
        for to_ref, from_ref in zip((acc_ref, max_ref, sum_ref), state_refs):
            to_ref[...] = from_ref[...]

    def body(b, j, q_rows, all_rows, hidden):
        every = [slice(h * HD, (h + 1) * HD) for h in range(heads)]
        key = [kv_refs[j][:, cols] for cols in every]
        value = [kv_refs[j][:, width + h * HD : width + (h + 1) * HD] for h in range(heads)]
        old = [max_ref[h : h + 1, all_rows] for h in range(heads)]
        scores = [dot(key[h], query_refs[b][q_rows, cols], NT) * SCALE2 for h, cols in enumerate(every)]
        if hidden is not None:
            scores = [jnp.where(hidden, HIDDEN, score) for score in scores]
        new = [jnp.maximum(m, jnp.max(x, axis=0, keepdims=True)) for m, x in zip(old, scores)]
        weights = [jnp.exp2(x - m) for x, m in zip(scores, new)]
        fades = [jnp.exp2(m - n) for m, n in zip(old, new)]
        sums = [
            sum_ref[h : h + 1, all_rows] * fades[h] + jnp.sum(weights[h], axis=0, keepdims=True)
            for h in range(heads)
        ]
        mixes = [dot(v, w.astype(BF16), TN) for v, w in zip(value, weights)]
        for h, cols in enumerate(every):
            max_ref[h : h + 1, all_rows] = new[h]
            sum_ref[h : h + 1, all_rows] = sums[h]
            acc_ref[cols, all_rows] = acc_ref[cols, all_rows] * fades[h] + mixes[h]

    for_pairs(body, limit_ref, span_ref, base_ref, slab, pairs)
    if not last:
        return
    total = jnp.maximum(sum_ref[...], 1e-30)
    lse = max_ref[...] + jnp.log2(total)
    own_lse_ref[...] = lse[:, :rows]
    peer_lse_ref[...] = lse[:, rows:]
    for b, out_ref in enumerate((own_ref, peer_ref)):
        for s in range(2):
            at = slice((2 * b + s) * slab, (2 * b + s + 1) * slab)
            for h in range(heads):
                cols = slice(h * HD, (h + 1) * HD)
                mixed = acc_ref[cols, at] / total[h : h + 1, at]
                out_ref[s * slab : (s + 1) * slab, cols] = mixed.T.astype(out_ref.dtype)


def merge_kernel(heads, slab, own_ref, own_lse_ref, from_ref, from_lse_ref, dout_ref, mixed_ref, stats_ref):
    a, b = own_lse_ref[...], from_lse_ref[...]
    top = jnp.maximum(a, b)
    lse = top + jnp.log2(jnp.exp2(a - top) + jnp.exp2(b - top))
    stats_ref[...] = lse
    share_a, share_b = jnp.exp2(a - lse), jnp.exp2(b - lse)
    for s in range(2):
        at = slice(s * slab, (s + 1) * slab)
        for h in range(heads):
            cols = slice(h * HD, (h + 1) * HD)
            wa = jnp.broadcast_to(share_a[h : h + 1, at], (HD, slab)).T
            wb = jnp.broadcast_to(share_b[h : h + 1, at], (HD, slab)).T
            mixed = (own_ref[at, cols] * wa + from_ref[at, cols].astype(F32) * wb).astype(BF16)
            mixed_ref[at, cols] = mixed
            prod = mixed.astype(F32) * dout_ref[at, cols].astype(F32)
            stats_ref[heads + h : heads + h + 1, at] = jnp.sum(prod.T, axis=0, keepdims=True)


def backward_kernel(keys, heads, slab, first, last, *refs):
    facts_ref, *refs = refs
    n_key = len(keys)
    query_refs, dout_refs, stat_refs, refs = refs[:2], refs[2:4], refs[4:6], refs[6:]
    kv_refs, refs = refs[:n_key], refs[n_key:]
    state_refs, refs = ([], refs) if first else (refs[:1], refs[1:])
    dkv_refs, refs = refs[: n_key // 2], refs[n_key // 2 :]
    if last:
        own_ref, peer_ref, *refs = refs
    dq_ref, dk_ref, dv_ref, limit_ref, span_ref, base_ref = refs
    rows, width = 2 * slab, heads * HD
    visibility(facts_ref, limit_ref, span_ref, base_ref, slab, keys)
    if first:
        dq_ref[...] = jnp.zeros_like(dq_ref)
    else:
        dq_ref[...] = state_refs[0][...]
    dk_ref[...] = jnp.zeros_like(dk_ref)
    dv_ref[...] = jnp.zeros_like(dv_ref)

    def body(b, j, q_rows, all_rows, hidden):
        every = [slice(h * HD, (h + 1) * HD) for h in range(heads)]
        query = [query_refs[b][q_rows, cols] for cols in every]
        dout = [dout_refs[b][q_rows, cols] for cols in every]
        lse = [stat_refs[b][h : h + 1, q_rows] for h in range(heads)]
        row_dot = [stat_refs[b][heads + h : heads + h + 1, q_rows] for h in range(heads)]
        key = [kv_refs[j][:, cols] for cols in every]
        value = [kv_refs[j][:, width + h * HD : width + (h + 1) * HD] for h in range(heads)]
        scores = [dot(key[h], query[h], NT) * SCALE2 for h in range(heads)]
        weights = [jnp.exp2(scores[h] - lse[h]) for h in range(heads)]
        if hidden is not None:
            weights = [jnp.where(hidden, 0.0, weight) for weight in weights]
        d_weights = [dot(value[h], dout[h], NT) for h in range(heads)]
        d_scores = [(weights[h] * (d_weights[h] - row_dot[h])).astype(BF16) for h in range(heads)]
        add_v = [dot(weights[h].astype(BF16), dout[h], NN) for h in range(heads)]
        add_k = [dot(d_scores[h], query[h], NN) for h in range(heads)]
        add_q = [dot(key[h], d_scores[h], TN) for h in range(heads)]
        for h, cols in enumerate(every):
            dv_ref[j, :, cols] += add_v[h]
            dk_ref[j, :, cols] += add_k[h]
            dq_ref[cols, all_rows] += add_q[h]

    pairs = [(j, b) for j in range(n_key) for b in range(2)]
    for_pairs(body, limit_ref, span_ref, base_ref, slab, pairs)
    for j in range(n_key):
        at = slice(j % 2 * slab, (j % 2 + 1) * slab)
        dkv_refs[j // 2][at, :width] = (dk_ref[j] * SCALE).astype(BF16)
        dkv_refs[j // 2][at, width:] = dv_ref[j].astype(BF16)
    if not last:
        return
    for b, out_ref in enumerate((own_ref, peer_ref)):
        for s in range(2):
            at = slice((2 * b + s) * slab, (2 * b + s + 1) * slab)
            for h in range(heads):
                cols = slice(h * HD, (h + 1) * HD)
                out_ref[s * slab : (s + 1) * slab, cols] = (dq_ref[cols, at] * SCALE).T.astype(out_ref.dtype)


def grad_kernel(steps, grad_hbm, w_hbm, out_ref, grad_ref, w_ref, grad_sem, w_sem):
    tile = grad_ref.shape[2]
    copies = []
    for k in range(steps):
        at = pl.ds(k * tile, tile)
        copies.append(
            (
                pltpu.make_async_copy(grad_hbm.at[:, at], grad_ref.at[k], grad_sem.at[k]),
                pltpu.make_async_copy(w_hbm.at[:, at], w_ref.at[k], w_sem.at[k]),
            )
        )
        for copy in copies[-1]:
            copy.start()
    total = None
    for k in range(steps):
        for copy in copies[k]:
            copy.wait()
        part = dot(grad_ref[k], w_ref[k], NT)
        total = part if total is None else total + part
    out_ref[...] = total.astype(BF16)


def project_grad(grad_rows, w_out, tile):
    rows, width, steps = grad_rows.shape[0], w_out.shape[0], w_out.shape[1] // tile
    hbm = pl.BlockSpec(memory_space=pltpu.MemorySpace.HBM)
    return pl.pallas_call(
        functools.partial(grad_kernel, steps),
        out_shape=jax.ShapeDtypeStruct((rows, width), BF16),
        in_specs=[hbm, hbm],
        out_specs=VMEM,
        scratch_shapes=[
            pltpu.VMEM((steps, rows, tile), BF16),
            pltpu.VMEM((steps, width, tile), BF16),
            pltpu.SemaphoreType.DMA((steps,)),
            pltpu.SemaphoreType.DMA((steps,)),
        ],
        compiler_params=pltpu.CompilerParams(vmem_limit_bytes=20 * 2**20),
        cost_estimate=CHEAP,
        name="project_grad",
    )(in_hbm(grad_rows), in_hbm(w_out))


def out_kernel(steps, at_ref, mixed_ref, other_ref, w_hbm, w_there_hbm, out_hbm, pair_ref, w_ref, out_ref, sems):
    width, tile = mixed_ref.shape[1], w_ref.shape[2]
    loads, stores = [], []
    for k in range(steps):
        cols = pl.ds(pl.multiple_of((at_ref[0] * steps + k) * tile, tile), tile)
        pair = [
            pltpu.make_async_copy(hbm.at[:, cols], w_ref.at[k, pl.ds(part * width, width), :], sems.at[part, k])
            for part, hbm in enumerate((w_hbm, w_there_hbm))
        ]
        for load in pair:
            load.start()
        loads.append(pair)
        stores.append(
            pltpu.make_async_copy(out_ref.at[k], out_hbm.at[:, pl.ds(k * tile, tile)], sems.at[2, k])
        )
    pair_ref[:, :width] = mixed_ref[...]
    pair_ref[:, width:] = other_ref[...]
    for k in range(steps):
        for load in loads[k]:
            load.wait()
        out_ref[k] = dot(pair_ref[...], w_ref[k], NN).astype(BF16)
        stores[k].start()
    for store in stores:
        store.wait()


def project_out(core, mixed, other, w_out, w_there, tile):
    (rows, width), half = mixed.shape, w_there.shape[1] // 2
    steps = half // tile
    hbm = pl.BlockSpec(memory_space=pltpu.MemorySpace.HBM)
    return pl.pallas_call(
        functools.partial(out_kernel, steps),
        out_shape=pltpu.MemorySpace.HBM((rows, half), BF16),
        in_specs=[SMEM, VMEM, VMEM, hbm, hbm],
        out_specs=hbm,
        scratch_shapes=[
            pltpu.VMEM((rows, 2 * width), BF16),
            pltpu.VMEM((steps, 2 * width, tile), BF16),
            pltpu.VMEM((steps, rows, tile), BF16),
            pltpu.SemaphoreType.DMA((3, steps)),
        ],
        compiler_params=pltpu.CompilerParams(vmem_limit_bytes=20 * 2**20),
        cost_estimate=CHEAP,
        name="project_out",
    )(core.reshape(1).astype(jnp.int32), mixed, other, in_hbm(w_out), in_hbm(w_there))


CHEAP = pl.CostEstimate(flops=1, bytes_accessed=1, transcendentals=0)
SMEM = pl.BlockSpec(memory_space=pltpu.SMEM)
VMEM = pl.BlockSpec(memory_space=pltpu.VMEM)
LIMIT = 16 * 2**20


def add_kernel(a_ref, b_ref, out_ref):
    out_ref[...] = (a_ref[...].astype(F32) + b_ref[...].astype(F32)).astype(out_ref.dtype)


def kv_kernel(early_ref, next_ref, prev_ref, k_ref, v_ref):
    width = k_ref.shape[1]
    for out_ref, cols in ((k_ref, slice(0, width)), (v_ref, slice(width, 2 * width))):
        total = early_ref[:, cols] + next_ref[:, cols].astype(F32) + prev_ref[:, cols].astype(F32)
        out_ref[...] = total.astype(BF16)


def part_kernel(at_ref, rows_ref, out_ref):
    few = out_ref.shape[0]
    out_ref[...] = rows_ref[pl.ds(pl.multiple_of(at_ref[0] * few, few), few), :]


def out_sum_kernel(at_ref, rows_ref, from_ref, here_ref, there_ref):
    few = here_ref.shape[0]
    for out_ref, core in ((here_ref, at_ref[1]), (there_ref, 1 - at_ref[1])):
        mine = rows_ref[pl.ds(pl.multiple_of((at_ref[0] * 2 + core) * few, few), few), :]
        other = from_ref[pl.ds(pl.multiple_of(core * few, few), few), :]
        out_ref[...] = (mine.astype(F32) + other.astype(F32)).astype(BF16)


def call(kernel, outs, n_scalar, n_vector, scratch, name, flops=1):
    return pl.pallas_call(
        kernel,
        out_shape=[jax.ShapeDtypeStruct(shape, dtype) for shape, dtype in outs],
        in_specs=[SMEM] * n_scalar + [VMEM] * n_vector,
        out_specs=[VMEM] * len(outs),
        scratch_shapes=scratch,
        compiler_params=pltpu.CompilerParams(vmem_limit_bytes=LIMIT),
        cost_estimate=pl.CostEstimate(flops=flops, bytes_accessed=1, transcendentals=0),
        name=name,
    )


def on_device(queries, keys, values, w_out, grad_out, slab_order, frame_lengths):
    rows, width = queries.shape
    heads, slab = width // HD, rows // 2
    n_head = lax.axis_size("head")
    half = w_out.shape[1] // 2
    ctx, head = lax.axis_index("ctx"), lax.axis_index("head")
    core = head % 2

    def over_x(array, o):
        perm = [(y * 4 + x, y * 4 + (x - o) % 4) for y in range(2) for x in range(4)]
        return lax.ppermute(array, "ctx", perm)

    def over_y(array):
        return lax.ppermute(array, "ctx", [(c, (c + 4) % 8) for c in range(8)])

    def over_core(array):
        return lax.ppermute(array, "head", [(h, h ^ 1) for h in range(n_head)])

    def over_chips(array, dz, dy):
        perm = [(h, ((h // 4 + dz) % 4) * 4 + (h ^ (2 * dy)) % 4) for h in range(n_head)]
        return lax.ppermute(array, "head", perm)

    offsets = (0, 1, 3, 2)
    base = ctx // 4 * 4
    slots = [(base + (ctx + o) % 4) * 2 + s for o in offsets for s in range(2)]
    places = jnp.stack([ctx, (ctx + 4) % 8] + slots).astype(jnp.int32)
    facts = jnp.concatenate([places, slab_order, frame_lengths])
    part = (rows, width)
    stat = (8, rows)

    def masks(n_key):
        return [
            pltpu.VMEM((1, 2 * rows), jnp.int32),
            pltpu.SMEM((4, 2), jnp.int32),
            pltpu.SMEM((n_key,), jnp.int32),
        ]

    def forward(keys, pairs, state, last):
        n_key, n_query = len(keys), 1 + max(b for _, b in pairs)
        states = [((width, 2 * rows), F32), ((8, 2 * rows), F32), ((8, 2 * rows), F32)]
        results = [(part, F32), (stat, F32), (part, BF16), (stat, F32)]
        return call(
            functools.partial(forward_kernel, keys, pairs, heads, slab, not state, last),
            results if last else states,
            1,
            n_query + n_key + len(state),
            [pltpu.VMEM(*s) for s in states if last] + masks(n_key),
            "forward",
        )(facts, *(queries, peer_queries)[:n_query], *(kv[k] for k in keys), *state)

    def backward(keys, state, last):
        n_key, n_block = len(keys), len(keys) // 2
        states = [((width, 2 * rows), F32)]
        results = [(part, F32), (part, BF16)]
        scratch = [
            pltpu.VMEM((n_key, slab, width), F32),
            pltpu.VMEM((n_key, slab, width), F32),
        ]
        outs = call(
            functools.partial(backward_kernel, keys, heads, slab, not state, last),
            [((rows, 2 * width), BF16)] * n_block + (results if last else states),
            1,
            6 + n_key + len(state),
            [pltpu.VMEM(*s) for s in states if last] + scratch + masks(n_key),
            "backward",
        )(
            facts,
            queries,
            peer_queries,
            grad_mixed,
            peer_grad,
            stats,
            peer_stats,
            *(in_hbm(kv[k]) for k in keys),
            *(in_hbm(array) for array in state),
        )
        return outs[:n_block], outs[n_block:]

    peer_queries = over_y(queries)
    kv = [jnp.concatenate([keys[at], values[at]], axis=1) for at in (slice(0, slab), slice(slab, rows))]
    next_0, prev_1 = over_x(kv[0], 1), over_x(kv[1], 3)
    next_1, prev_0 = over_x(kv[1], 1), over_x(kv[0], 3)
    grad_rows = lax.all_gather(grad_out, "head", axis=0, tiled=True)
    w_there = over_core(w_out)
    state = forward((0, 1), ((0, 0), (1, 0)), [], False)
    next_0, prev_1, *state = lax.optimization_barrier((next_0, prev_1, *state))
    kv += [next_0, next_1, prev_0, prev_1, over_x(next_0, 1), over_x(prev_1, 3)]
    w_there, *state = lax.optimization_barrier((w_there, *state))
    state = forward((0, 1, 2, 5), ((0, 1), (1, 1), (2, 0), (2, 1), (3, 0), (3, 1)), state, False)
    every = tuple((j, b) for j in range(2) for b in range(2))
    state = forward((3, 4), every, state, False)
    own_mixed, own_lse, peer_mixed, peer_lse = forward((6, 7), every, state, True)
    from_lse, from_mixed = over_y(peer_lse), over_y(peer_mixed)

    grad_rows, peer_lse = lax.optimization_barrier((grad_rows, peer_lse))
    grad_mixed = project_grad(grad_rows, w_out, 1024)
    peer_grad = over_y(grad_mixed)
    mixed, stats = call(
        functools.partial(merge_kernel, heads, slab),
        [(part, BF16), (stat, F32)],
        0,
        5,
        [],
        "merge",
    )(in_hbm(own_mixed), in_hbm(own_lse), from_mixed, in_hbm(from_lse), grad_mixed)
    peer_stats = over_y(stats)

    out_part = project_out(core, mixed, over_core(mixed), w_out, w_there, 512)
    z_groups = [[z * 4 + r for z in range(4)] for r in range(4)]
    out_part, peer_grad, peer_stats = lax.optimization_barrier((out_part, peer_grad, peer_stats))
    out_rows = lax.psum_scatter(
        out_part, "head", scatter_dimension=0, tiled=True, axis_index_groups=z_groups
    )

    (far_dkv,), state = backward((6, 7), [], False)
    far_dkv = over_x(far_dkv, 2)
    (next_dkv, prev_dkv), state = backward((2, 3, 4, 5), state, False)
    next_dkv, prev_dkv = over_x(next_dkv, 3), over_x(prev_dkv, 1)
    (own_dkv,), (own_dq, peer_dq) = backward((0, 1), state, True)
    peer_dq = over_y(peer_dq)

    own_dkv, far_dkv = lax.optimization_barrier((own_dkv, far_dkv))
    short = 3 * 10**8
    (kv_early,) = call(add_kernel, [((rows, 2 * width), F32)], 0, 2, [], "kv_early", short)(
        in_hbm(own_dkv), far_dkv
    )
    kv_early, next_dkv, prev_dkv = lax.optimization_barrier((kv_early, next_dkv, prev_dkv))
    k_grad, v_grad = call(kv_kernel, [(part, BF16)] * 2, 0, 3, [], "kv_sum")(kv_early, next_dkv, prev_dkv)
    own_dq, peer_dq, k_grad = lax.optimization_barrier((own_dq, peer_dq, k_grad))
    (q_grad,) = call(add_kernel, [(part, BF16)], 0, 2, [], "q_sum", short)(own_dq, peer_dq)

    few = 2 * rows // n_head // 2
    y_lo = head // 2 % 2
    spot = jnp.stack([y_lo, core]).astype(jnp.int32)
    (to_send,) = call(part_kernel, [((2 * few, half), BF16)], 1, 1, [], "out_piece")(1 - spot, in_hbm(out_rows))
    received = over_chips(to_send, 0, 1)
    received, k_grad, q_grad = lax.optimization_barrier((received, k_grad, q_grad))
    here, there = call(out_sum_kernel, [((few, half), BF16)] * 2, 1, 2, [], "out_sum")(spot, in_hbm(out_rows), received)
    there = over_core(there)
    layer_out = jnp.concatenate(
        [jnp.where(core == 0, here, there), jnp.where(core == 0, there, here)], axis=1
    )
    return layer_out, q_grad, k_grad, v_grad


def solution(mesh):
    in_specs = (
        P("ctx", "head"),
        P("ctx", "head"),
        P("ctx", "head"),
        P("head", None),
        P(("ctx", "head"), None),
        P(),
        P(),
    )
    out_specs = (P(("ctx", "head"), None), P("ctx", "head"), P("ctx", "head"), P("ctx", "head"))
    return jax.shard_map(on_device, mesh=mesh, in_specs=in_specs, out_specs=out_specs, check_vma=False)
```

```python
import functools
import math

import jax
import jax.numpy as jnp
from jax import lax
from jax.experimental import pallas as pl
from jax.experimental.pallas import tpu as pltpu
from jax.sharding import PartitionSpec as P

HD = 128
LOG2E = math.log2(math.e)
SCALE = float(HD) ** -0.5
SCALE2 = SCALE * LOG2E
START_MAX = -1e20
HIDDEN = -1e30
F32, BF16 = jnp.float32, jnp.bfloat16
NT = (((1,), (1,)), ((), ()))
TN = (((0,), (0,)), ((), ()))
NN = (((1,), (0,)), ((), ()))


def in_hbm(array):
    return pltpu.with_memory_space_constraint(array, pltpu.MemorySpace.HBM)


def dot(a, b, dims):
    return lax.dot_general(a, b, dims, preferred_element_type=F32)


def last_visible(ends, pos):
    limit = ends[-1]
    for end in reversed(ends[:-1]):
        limit = jnp.where(end > pos, end, limit)
    return limit


def visibility(facts_ref, limit_ref, span_ref, base_ref, slab, keys):
    n_slot = 8
    order, length = 2 + n_slot, 2 + n_slot + (facts_ref.shape[0] - 2 - n_slot) // 2
    ends, total = [], jnp.int32(0)
    for f in range(length, facts_ref.shape[0]):
        total = total + facts_ref[f]
        ends.append(total)
    for i in range(4):
        base = facts_ref[order + facts_ref[i // 2] * 2 + i % 2] * slab
        rows = base + lax.broadcasted_iota(jnp.int32, (1, slab), 1)
        limit_ref[:, i * slab : (i + 1) * slab] = last_visible(ends, rows)
        span_ref[i, 0] = last_visible(ends, base)
        span_ref[i, 1] = last_visible(ends, base + slab - 1)
    for j, key in enumerate(keys):
        base_ref[j] = facts_ref[order + facts_ref[2 + key]] * slab


def for_pairs(body, limit_ref, span_ref, base_ref, slab, pairs):
    for j, b in pairs:

        def step(i, carry, b=b, j=j):
            base = base_ref[j]
            low, high = span_ref[2 * b + i, 0], span_ref[2 * b + i, 1]
            q_rows = pl.ds(pl.multiple_of(i * slab, slab), slab)
            all_rows = pl.ds(pl.multiple_of((2 * b + i) * slab, slab), slab)

            @pl.when(base + slab <= low)
            def _():
                body(b, j, q_rows, all_rows, None)

            @pl.when(jnp.logical_and(base < high, base + slab > low))
            def _():
                limit = limit_ref[:, all_rows] - base
                hidden = lax.broadcasted_iota(jnp.int32, (slab, slab), 0) >= limit
                body(b, j, q_rows, all_rows, hidden)

            return carry

        lax.fori_loop(0, 2, step, 0)


def forward_kernel(keys, pairs, heads, slab, first, last, *refs):
    facts_ref, *refs = refs
    n_key = len(keys)
    n_query = 1 + max(b for _, b in pairs)
    query_refs, refs = refs[:n_query], refs[n_query:]
    kv_refs, refs = refs[:n_key], refs[n_key:]
    state_refs, refs = ([], refs) if first else (refs[:3], refs[3:])
    if last:
        own_ref, own_lse_ref, peer_ref, peer_lse_ref, *refs = refs
    acc_ref, max_ref, sum_ref, limit_ref, span_ref, base_ref = refs
    rows, width = 2 * slab, heads * HD
    visibility(facts_ref, limit_ref, span_ref, base_ref, slab, keys)
    if first:
        acc_ref[...] = jnp.zeros_like(acc_ref)
        max_ref[...] = jnp.full_like(max_ref, START_MAX)
        sum_ref[...] = jnp.zeros_like(sum_ref)
    else:
        for to_ref, from_ref in zip((acc_ref, max_ref, sum_ref), state_refs):
            to_ref[...] = from_ref[...]

    def body(b, j, q_rows, all_rows, hidden):
        every = [slice(h * HD, (h + 1) * HD) for h in range(heads)]
        key = [kv_refs[j][:, cols] for cols in every]
        value = [kv_refs[j][:, width + h * HD : width + (h + 1) * HD] for h in range(heads)]
        old = [max_ref[h : h + 1, all_rows] for h in range(heads)]
        scores = [dot(key[h], query_refs[b][q_rows, cols], NT) * SCALE2 for h, cols in enumerate(every)]
        if hidden is not None:
            scores = [jnp.where(hidden, HIDDEN, score) for score in scores]
        new = [jnp.maximum(m, jnp.max(x, axis=0, keepdims=True)) for m, x in zip(old, scores)]
        weights = [jnp.exp2(x - m) for x, m in zip(scores, new)]
        fades = [jnp.exp2(m - n) for m, n in zip(old, new)]
        sums = [
            sum_ref[h : h + 1, all_rows] * fades[h] + jnp.sum(weights[h], axis=0, keepdims=True)
            for h in range(heads)
        ]
        mixes = [dot(v, w.astype(BF16), TN) for v, w in zip(value, weights)]
        for h, cols in enumerate(every):
            max_ref[h : h + 1, all_rows] = new[h]
            sum_ref[h : h + 1, all_rows] = sums[h]
            acc_ref[cols, all_rows] = acc_ref[cols, all_rows] * fades[h] + mixes[h]

    for_pairs(body, limit_ref, span_ref, base_ref, slab, pairs)
    if not last:
        return
    total = jnp.maximum(sum_ref[...], 1e-30)
    lse = max_ref[...] + jnp.log2(total)
    own_lse_ref[...] = lse[:, :rows]
    peer_lse_ref[...] = lse[:, rows:]
    for b, out_ref in enumerate((own_ref, peer_ref)):
        for s in range(2):
            at = slice((2 * b + s) * slab, (2 * b + s + 1) * slab)
            for h in range(heads):
                cols = slice(h * HD, (h + 1) * HD)
                mixed = acc_ref[cols, at] / total[h : h + 1, at]
                out_ref[s * slab : (s + 1) * slab, cols] = mixed.T.astype(out_ref.dtype)


def merge_kernel(heads, slab, own_ref, own_lse_ref, from_ref, from_lse_ref, dout_ref, mixed_ref, stats_ref):
    a, b = own_lse_ref[...], from_lse_ref[...]
    top = jnp.maximum(a, b)
    lse = top + jnp.log2(jnp.exp2(a - top) + jnp.exp2(b - top))
    stats_ref[...] = lse
    share_a, share_b = jnp.exp2(a - lse), jnp.exp2(b - lse)
    for s in range(2):
        at = slice(s * slab, (s + 1) * slab)
        for h in range(heads):
            cols = slice(h * HD, (h + 1) * HD)
            wa = jnp.broadcast_to(share_a[h : h + 1, at], (HD, slab)).T
            wb = jnp.broadcast_to(share_b[h : h + 1, at], (HD, slab)).T
            mixed = (own_ref[at, cols] * wa + from_ref[at, cols].astype(F32) * wb).astype(BF16)
            mixed_ref[at, cols] = mixed
            prod = mixed.astype(F32) * dout_ref[at, cols].astype(F32)
            stats_ref[heads + h : heads + h + 1, at] = jnp.sum(prod.T, axis=0, keepdims=True)


def backward_kernel(keys, heads, slab, first, last, *refs):
    facts_ref, *refs = refs
    n_key = len(keys)
    query_refs, dout_refs, stat_refs, refs = refs[:2], refs[2:4], refs[4:6], refs[6:]
    kv_refs, refs = refs[:n_key], refs[n_key:]
    state_refs, refs = ([], refs) if first else (refs[:1], refs[1:])
    dkv_refs, refs = refs[: n_key // 2], refs[n_key // 2 :]
    if last:
        own_ref, peer_ref, *refs = refs
    dq_ref, dk_ref, dv_ref, limit_ref, span_ref, base_ref = refs
    rows, width = 2 * slab, heads * HD
    visibility(facts_ref, limit_ref, span_ref, base_ref, slab, keys)
    if first:
        dq_ref[...] = jnp.zeros_like(dq_ref)
    else:
        dq_ref[...] = state_refs[0][...]
    dk_ref[...] = jnp.zeros_like(dk_ref)
    dv_ref[...] = jnp.zeros_like(dv_ref)

    def body(b, j, q_rows, all_rows, hidden):
        every = [slice(h * HD, (h + 1) * HD) for h in range(heads)]
        query = [query_refs[b][q_rows, cols] for cols in every]
        dout = [dout_refs[b][q_rows, cols] for cols in every]
        lse = [stat_refs[b][h : h + 1, q_rows] for h in range(heads)]
        row_dot = [stat_refs[b][heads + h : heads + h + 1, q_rows] for h in range(heads)]
        key = [kv_refs[j][:, cols] for cols in every]
        value = [kv_refs[j][:, width + h * HD : width + (h + 1) * HD] for h in range(heads)]
        scores = [dot(key[h], query[h], NT) * SCALE2 for h in range(heads)]
        weights = [jnp.exp2(scores[h] - lse[h]) for h in range(heads)]
        if hidden is not None:
            weights = [jnp.where(hidden, 0.0, weight) for weight in weights]
        d_weights = [dot(value[h], dout[h], NT) for h in range(heads)]
        d_scores = [(weights[h] * (d_weights[h] - row_dot[h])).astype(BF16) for h in range(heads)]
        add_v = [dot(weights[h].astype(BF16), dout[h], NN) for h in range(heads)]
        add_k = [dot(d_scores[h], query[h], NN) for h in range(heads)]
        add_q = [dot(key[h], d_scores[h], TN) for h in range(heads)]
        for h, cols in enumerate(every):
            dv_ref[j, :, cols] += add_v[h]
            dk_ref[j, :, cols] += add_k[h]
            dq_ref[cols, all_rows] += add_q[h]

    pairs = [(j, b) for j in range(n_key) for b in range(2)]
    for_pairs(body, limit_ref, span_ref, base_ref, slab, pairs)
    for j in range(n_key):
        at = slice(j % 2 * slab, (j % 2 + 1) * slab)
        dkv_refs[j // 2][at, :width] = (dk_ref[j] * SCALE).astype(BF16)
        dkv_refs[j // 2][at, width:] = dv_ref[j].astype(BF16)
    if not last:
        return
    for b, out_ref in enumerate((own_ref, peer_ref)):
        for s in range(2):
            at = slice((2 * b + s) * slab, (2 * b + s + 1) * slab)
            for h in range(heads):
                cols = slice(h * HD, (h + 1) * HD)
                out_ref[s * slab : (s + 1) * slab, cols] = (dq_ref[cols, at] * SCALE).T.astype(out_ref.dtype)


def grad_kernel(steps, grad_hbm, w_hbm, out_ref, grad_ref, w_ref, grad_sem, w_sem):
    tile = grad_ref.shape[2]
    copies = []
    for k in range(steps):
        at = pl.ds(k * tile, tile)
        copies.append(
            (
                pltpu.make_async_copy(grad_hbm.at[:, at], grad_ref.at[k], grad_sem.at[k]),
                pltpu.make_async_copy(w_hbm.at[:, at], w_ref.at[k], w_sem.at[k]),
            )
        )
        for copy in copies[-1]:
            copy.start()
    total = None
    for k in range(steps):
        for copy in copies[k]:
            copy.wait()
        part = dot(grad_ref[k], w_ref[k], NT)
        total = part if total is None else total + part
    out_ref[...] = total.astype(BF16)


def project_grad(grad_rows, w_out, tile):
    rows, width, steps = grad_rows.shape[0], w_out.shape[0], w_out.shape[1] // tile
    hbm = pl.BlockSpec(memory_space=pltpu.MemorySpace.HBM)
    return pl.pallas_call(
        functools.partial(grad_kernel, steps),
        out_shape=jax.ShapeDtypeStruct((rows, width), BF16),
        in_specs=[hbm, hbm],
        out_specs=VMEM,
        scratch_shapes=[
            pltpu.VMEM((steps, rows, tile), BF16),
            pltpu.VMEM((steps, width, tile), BF16),
            pltpu.SemaphoreType.DMA((steps,)),
            pltpu.SemaphoreType.DMA((steps,)),
        ],
        compiler_params=pltpu.CompilerParams(vmem_limit_bytes=20 * 2**20),
        cost_estimate=CHEAP,
        name="project_grad",
    )(in_hbm(grad_rows), in_hbm(w_out))


def out_kernel(steps, at_ref, mixed_ref, other_ref, w_hbm, w_there_hbm, out_hbm, pair_ref, w_ref, out_ref, sems):
    width, tile = mixed_ref.shape[1], w_ref.shape[2]
    loads, stores = [], []
    for k in range(steps):
        cols = pl.ds(pl.multiple_of((at_ref[0] * steps + k) * tile, tile), tile)
        pair = [
            pltpu.make_async_copy(hbm.at[:, cols], w_ref.at[k, pl.ds(part * width, width), :], sems.at[part, k])
            for part, hbm in enumerate((w_hbm, w_there_hbm))
        ]
        for load in pair:
            load.start()
        loads.append(pair)
        stores.append(
            pltpu.make_async_copy(out_ref.at[k], out_hbm.at[:, pl.ds(k * tile, tile)], sems.at[2, k])
        )
    pair_ref[:, :width] = mixed_ref[...]
    pair_ref[:, width:] = other_ref[...]
    for k in range(steps):
        for load in loads[k]:
            load.wait()
        out_ref[k] = dot(pair_ref[...], w_ref[k], NN).astype(BF16)
        stores[k].start()
    for store in stores:
        store.wait()


def project_out(core, mixed, other, w_out, w_there, tile):
    (rows, width), half = mixed.shape, w_there.shape[1] // 2
    steps = half // tile
    hbm = pl.BlockSpec(memory_space=pltpu.MemorySpace.HBM)
    return pl.pallas_call(
        functools.partial(out_kernel, steps),
        out_shape=pltpu.MemorySpace.HBM((rows, half), BF16),
        in_specs=[SMEM, VMEM, VMEM, hbm, hbm],
        out_specs=hbm,
        scratch_shapes=[
            pltpu.VMEM((rows, 2 * width), BF16),
            pltpu.VMEM((steps, 2 * width, tile), BF16),
            pltpu.VMEM((steps, rows, tile), BF16),
            pltpu.SemaphoreType.DMA((3, steps)),
        ],
        compiler_params=pltpu.CompilerParams(vmem_limit_bytes=20 * 2**20),
        cost_estimate=CHEAP,
        name="project_out",
    )(core.reshape(1).astype(jnp.int32), mixed, other, in_hbm(w_out), in_hbm(w_there))


CHEAP = pl.CostEstimate(flops=1, bytes_accessed=1, transcendentals=0)
SMEM = pl.BlockSpec(memory_space=pltpu.SMEM)
VMEM = pl.BlockSpec(memory_space=pltpu.VMEM)
LIMIT = 16 * 2**20


def add_kernel(a_ref, b_ref, out_ref):
    out_ref[...] = (a_ref[...].astype(F32) + b_ref[...].astype(F32)).astype(out_ref.dtype)


def kv_kernel(early_ref, next_ref, prev_ref, k_ref, v_ref):
    width = k_ref.shape[1]
    for out_ref, cols in ((k_ref, slice(0, width)), (v_ref, slice(width, 2 * width))):
        total = early_ref[:, cols] + next_ref[:, cols].astype(F32) + prev_ref[:, cols].astype(F32)
        out_ref[...] = total.astype(BF16)


def part_kernel(at_ref, rows_ref, out_ref):
    few = out_ref.shape[0]
    out_ref[...] = rows_ref[pl.ds(pl.multiple_of(at_ref[0] * few, few), few), :]


def out_sum_kernel(at_ref, rows_ref, from_ref, here_ref, there_ref):
    few = here_ref.shape[0]
    for out_ref, core in ((here_ref, at_ref[1]), (there_ref, 1 - at_ref[1])):
        mine = rows_ref[pl.ds(pl.multiple_of((at_ref[0] * 2 + core) * few, few), few), :]
        other = from_ref[pl.ds(pl.multiple_of(core * few, few), few), :]
        out_ref[...] = (mine.astype(F32) + other.astype(F32)).astype(BF16)


def call(kernel, outs, n_scalar, n_vector, scratch, name, flops=1, to_hbm=()):
    return pl.pallas_call(
        kernel,
        out_shape=[
            (pltpu.MemorySpace.HBM if k in to_hbm else jax.ShapeDtypeStruct)(*out) for k, out in enumerate(outs)
        ],
        in_specs=[SMEM] * n_scalar + [VMEM] * n_vector,
        out_specs=[VMEM] * len(outs),
        scratch_shapes=scratch,
        compiler_params=pltpu.CompilerParams(vmem_limit_bytes=LIMIT),
        cost_estimate=pl.CostEstimate(flops=flops, bytes_accessed=1, transcendentals=0),
        name=name,
    )


def on_device(queries, keys, values, w_out, grad_out, slab_order, frame_lengths):
    rows, width = queries.shape
    heads, slab = width // HD, rows // 2
    n_head = lax.axis_size("head")
    half = w_out.shape[1] // 2
    ctx, head = lax.axis_index("ctx"), lax.axis_index("head")
    core = head % 2

    def over_x(array, o):
        perm = [(y * 4 + x, y * 4 + (x - o) % 4) for y in range(2) for x in range(4)]
        return lax.ppermute(array, "ctx", perm)

    def over_y(array):
        return lax.ppermute(array, "ctx", [(c, (c + 4) % 8) for c in range(8)])

    def over_core(array):
        return lax.ppermute(array, "head", [(h, h ^ 1) for h in range(n_head)])

    def over_chips(array, dz, dy):
        perm = [(h, ((h // 4 + dz) % 4) * 4 + (h ^ (2 * dy)) % 4) for h in range(n_head)]
        return lax.ppermute(array, "head", perm)

    offsets = (0, 1, 3, 2)
    base = ctx // 4 * 4
    slots = [(base + (ctx + o) % 4) * 2 + s for o in offsets for s in range(2)]
    places = jnp.stack([ctx, (ctx + 4) % 8] + slots).astype(jnp.int32)
    facts = jnp.concatenate([places, slab_order, frame_lengths])
    part = (rows, width)
    stat = (8, rows)

    def masks(n_key):
        return [
            pltpu.VMEM((1, 2 * rows), jnp.int32),
            pltpu.SMEM((4, 2), jnp.int32),
            pltpu.SMEM((n_key,), jnp.int32),
        ]

    def forward(keys, pairs, state, last):
        n_key, n_query = len(keys), 1 + max(b for _, b in pairs)
        states = [((width, 2 * rows), F32), ((8, 2 * rows), F32), ((8, 2 * rows), F32)]
        results = [(part, F32), (stat, F32), (part, BF16), (stat, F32)]
        return call(
            functools.partial(forward_kernel, keys, pairs, heads, slab, not state, last),
            results if last else states,
            1,
            n_query + n_key + len(state),
            [pltpu.VMEM(*s) for s in states if last] + masks(n_key),
            "forward",
            to_hbm=(0, 1) if last else (),
        )(facts, *(queries, peer_queries)[:n_query], *(in_hbm(kv[k]) for k in keys), *state)

    def backward(keys, state, last):
        n_key, n_block = len(keys), len(keys) // 2
        states = [((width, 2 * rows), F32)]
        results = [(part, F32), (part, BF16)]
        scratch = [
            pltpu.VMEM((n_key, slab, width), F32),
            pltpu.VMEM((n_key, slab, width), F32),
        ]
        outs = call(
            functools.partial(backward_kernel, keys, heads, slab, not state, last),
            [((rows, 2 * width), BF16)] * n_block + (results if last else states),
            1,
            6 + n_key + len(state),
            [pltpu.VMEM(*s) for s in states if last] + scratch + masks(n_key),
            "backward",
            to_hbm=(0,) if last else (n_block,),
        )(
            facts,
            queries,
            peer_queries,
            grad_mixed,
            peer_grad,
            stats,
            peer_stats,
            *(in_hbm(kv[k]) for k in keys),
            *(in_hbm(array) for array in state),
        )
        return outs[:n_block], outs[n_block:]

    peer_queries = over_y(queries)
    kv = [jnp.concatenate([keys[at], values[at]], axis=1) for at in (slice(0, slab), slice(slab, rows))]
    next_0, prev_1 = over_x(kv[0], 1), over_x(kv[1], 3)
    next_1, prev_0 = over_x(kv[1], 1), over_x(kv[0], 3)
    grad_rows = lax.all_gather(grad_out, "head", axis=0, tiled=True)
    w_there = over_core(w_out)
    state = forward((0, 1), ((0, 0), (1, 0)), [], False)
    next_0, prev_1, *state = lax.optimization_barrier((next_0, prev_1, *state))
    kv += [next_0, next_1, prev_0, prev_1, over_x(next_0, 1), over_x(prev_1, 3)]
    w_there, *state = lax.optimization_barrier((w_there, *state))
    state = forward((0, 1, 2, 5), ((0, 1), (1, 1), (2, 0), (2, 1), (3, 0), (3, 1)), state, False)
    every = tuple((j, b) for j in range(2) for b in range(2))
    state = forward((3, 4), every, state, False)
    own_mixed, own_lse, peer_mixed, peer_lse = forward((6, 7), every, state, True)
    from_lse, from_mixed = over_y(peer_lse), over_y(peer_mixed)

    grad_rows, peer_lse = lax.optimization_barrier((grad_rows, peer_lse))
    grad_mixed = project_grad(grad_rows, w_out, 1024)
    peer_grad = over_y(grad_mixed)
    mixed, stats = call(
        functools.partial(merge_kernel, heads, slab),
        [(part, BF16), (stat, F32)],
        0,
        5,
        [],
        "merge",
    )(in_hbm(own_mixed), in_hbm(own_lse), from_mixed, in_hbm(from_lse), grad_mixed)
    peer_stats = over_y(stats)

    out_part = project_out(core, mixed, over_core(mixed), w_out, w_there, 512)
    z_groups = [[z * 4 + r for z in range(4)] for r in range(4)]
    out_part, peer_grad, peer_stats = lax.optimization_barrier((out_part, peer_grad, peer_stats))
    out_rows = lax.psum_scatter(
        out_part, "head", scatter_dimension=0, tiled=True, axis_index_groups=z_groups
    )

    (far_dkv,), state = backward((6, 7), [], False)
    far_dkv = over_x(far_dkv, 2)
    (next_dkv, prev_dkv), state = backward((2, 3, 4, 5), state, False)
    next_dkv, prev_dkv = over_x(next_dkv, 3), over_x(prev_dkv, 1)
    (own_dkv,), (own_dq, peer_dq) = backward((0, 1), state, True)
    peer_dq = over_y(peer_dq)

    own_dkv, far_dkv = lax.optimization_barrier((own_dkv, far_dkv))
    short = 3 * 10**8
    (kv_early,) = call(add_kernel, [((rows, 2 * width), F32)], 0, 2, [], "kv_early", short)(
        in_hbm(own_dkv), far_dkv
    )
    kv_early, next_dkv, prev_dkv = lax.optimization_barrier((kv_early, next_dkv, prev_dkv))
    k_grad, v_grad = call(kv_kernel, [(part, BF16)] * 2, 0, 3, [], "kv_sum")(kv_early, next_dkv, prev_dkv)
    own_dq, peer_dq, k_grad = lax.optimization_barrier((own_dq, peer_dq, k_grad))
    (q_grad,) = call(add_kernel, [(part, BF16)], 0, 2, [], "q_sum", short)(own_dq, peer_dq)

    few = 2 * rows // n_head // 2
    y_lo = head // 2 % 2
    spot = jnp.stack([y_lo, core]).astype(jnp.int32)
    (to_send,) = call(part_kernel, [((2 * few, half), BF16)], 1, 1, [], "out_piece")(1 - spot, in_hbm(out_rows))
    received = over_chips(to_send, 0, 1)
    received, k_grad, q_grad = lax.optimization_barrier((received, k_grad, q_grad))
    here, there = call(out_sum_kernel, [((few, half), BF16)] * 2, 1, 2, [], "out_sum")(spot, in_hbm(out_rows), received)
    there = over_core(there)
    layer_out = jnp.concatenate(
        [jnp.where(core == 0, here, there), jnp.where(core == 0, there, here)], axis=1
    )
    return layer_out, q_grad, k_grad, v_grad


def solution(mesh):
    in_specs = (
        P("ctx", "head"),
        P("ctx", "head"),
        P("ctx", "head"),
        P("head", None),
        P(("ctx", "head"), None),
        P(),
        P(),
    )
    out_specs = (P(("ctx", "head"), None), P("ctx", "head"), P("ctx", "head"), P("ctx", "head"))
    return jax.shard_map(on_device, mesh=mesh, in_specs=in_specs, out_specs=out_specs, check_vma=False)
```

```python
import functools
import math

import jax
import jax.numpy as jnp
from jax import lax
from jax.experimental import pallas as pl
from jax.experimental.pallas import tpu as pltpu
from jax.sharding import PartitionSpec as P

HD = 128
LOG2E = math.log2(math.e)
SCALE = float(HD) ** -0.5
SCALE2 = SCALE * LOG2E
START_MAX = -1e20
HIDDEN = -1e30
F32, BF16 = jnp.float32, jnp.bfloat16
NT = (((1,), (1,)), ((), ()))
TN = (((0,), (0,)), ((), ()))
NN = (((1,), (0,)), ((), ()))


def in_hbm(array):
    return pltpu.with_memory_space_constraint(array, pltpu.MemorySpace.HBM)


def dot(a, b, dims):
    return lax.dot_general(a, b, dims, preferred_element_type=F32)


def last_visible(ends, pos):
    limit = ends[-1]
    for end in reversed(ends[:-1]):
        limit = jnp.where(end > pos, end, limit)
    return limit


def visibility(facts_ref, limit_ref, span_ref, base_ref, slab, keys):
    n_slot = 8
    order, length = 2 + n_slot, 2 + n_slot + (facts_ref.shape[0] - 2 - n_slot) // 2
    ends, total = [], jnp.int32(0)
    for f in range(length, facts_ref.shape[0]):
        total = total + facts_ref[f]
        ends.append(total)
    for i in range(4):
        base = facts_ref[order + facts_ref[i // 2] * 2 + i % 2] * slab
        rows = base + lax.broadcasted_iota(jnp.int32, (1, slab), 1)
        limit_ref[:, i * slab : (i + 1) * slab] = last_visible(ends, rows)
        span_ref[i, 0] = last_visible(ends, base)
        span_ref[i, 1] = last_visible(ends, base + slab - 1)
    for j, key in enumerate(keys):
        base_ref[j] = facts_ref[order + facts_ref[2 + key]] * slab


def for_pairs(body, limit_ref, span_ref, base_ref, slab, pairs):
    for j, b in pairs:

        def step(i, carry, b=b, j=j):
            base = base_ref[j]
            low, high = span_ref[2 * b + i, 0], span_ref[2 * b + i, 1]
            q_rows = pl.ds(pl.multiple_of(i * slab, slab), slab)
            all_rows = pl.ds(pl.multiple_of((2 * b + i) * slab, slab), slab)

            @pl.when(base + slab <= low)
            def _():
                body(b, j, q_rows, all_rows, None)

            @pl.when(jnp.logical_and(base < high, base + slab > low))
            def _():
                limit = limit_ref[:, all_rows] - base
                hidden = lax.broadcasted_iota(jnp.int32, (slab, slab), 0) >= limit
                body(b, j, q_rows, all_rows, hidden)

            return carry

        lax.fori_loop(0, 2, step, 0)


def forward_kernel(keys, pairs, heads, slab, first, last, *refs):
    facts_ref, *refs = refs
    n_key = len(keys)
    n_query = 1 + max(b for _, b in pairs)
    query_refs, refs = refs[:n_query], refs[n_query:]
    kv_refs, refs = refs[:n_key], refs[n_key:]
    state_refs, refs = ([], refs) if first else (refs[:3], refs[3:])
    if last:
        own_ref, own_lse_ref, peer_ref, peer_lse_ref, *refs = refs
    acc_ref, max_ref, sum_ref, limit_ref, span_ref, base_ref = refs
    rows, width = 2 * slab, heads * HD
    visibility(facts_ref, limit_ref, span_ref, base_ref, slab, keys)
    if first:
        acc_ref[...] = jnp.zeros_like(acc_ref)
        max_ref[...] = jnp.full_like(max_ref, START_MAX)
        sum_ref[...] = jnp.zeros_like(sum_ref)
    else:
        for to_ref, from_ref in zip((acc_ref, max_ref, sum_ref), state_refs):
            to_ref[...] = from_ref[...]

    def body(b, j, q_rows, all_rows, hidden):
        every = [slice(h * HD, (h + 1) * HD) for h in range(heads)]
        key = [kv_refs[j][:, cols] for cols in every]
        value = [kv_refs[j][:, width + h * HD : width + (h + 1) * HD] for h in range(heads)]
        old = [max_ref[h : h + 1, all_rows] for h in range(heads)]
        scores = [dot(key[h], query_refs[b][q_rows, cols], NT) * SCALE2 for h, cols in enumerate(every)]
        if hidden is not None:
            scores = [jnp.where(hidden, HIDDEN, score) for score in scores]
        new = [jnp.maximum(m, jnp.max(x, axis=0, keepdims=True)) for m, x in zip(old, scores)]
        weights = [jnp.exp2(x - m) for x, m in zip(scores, new)]
        fades = [jnp.exp2(m - n) for m, n in zip(old, new)]
        sums = [
            sum_ref[h : h + 1, all_rows] * fades[h] + jnp.sum(weights[h], axis=0, keepdims=True)
            for h in range(heads)
        ]
        mixes = [dot(v, w.astype(BF16), TN) for v, w in zip(value, weights)]
        for h, cols in enumerate(every):
            max_ref[h : h + 1, all_rows] = new[h]
            sum_ref[h : h + 1, all_rows] = sums[h]
            acc_ref[cols, all_rows] = acc_ref[cols, all_rows] * fades[h] + mixes[h]

    for_pairs(body, limit_ref, span_ref, base_ref, slab, pairs)
    if not last:
        return
    total = jnp.maximum(sum_ref[...], 1e-30)
    lse = max_ref[...] + jnp.log2(total)
    own_lse_ref[...] = lse[:, :rows]
    peer_lse_ref[...] = lse[:, rows:]
    for b, out_ref in enumerate((own_ref, peer_ref)):
        for s in range(2):
            at = slice((2 * b + s) * slab, (2 * b + s + 1) * slab)
            for h in range(heads):
                cols = slice(h * HD, (h + 1) * HD)
                mixed = acc_ref[cols, at] / total[h : h + 1, at]
                out_ref[s * slab : (s + 1) * slab, cols] = mixed.T.astype(out_ref.dtype)


def merge_kernel(heads, slab, own_ref, own_lse_ref, from_ref, from_lse_ref, dout_ref, mixed_ref, stats_ref):
    a, b = own_lse_ref[...], from_lse_ref[...]
    top = jnp.maximum(a, b)
    lse = top + jnp.log2(jnp.exp2(a - top) + jnp.exp2(b - top))
    stats_ref[...] = lse
    share_a, share_b = jnp.exp2(a - lse), jnp.exp2(b - lse)
    for s in range(2):
        at = slice(s * slab, (s + 1) * slab)
        for h in range(heads):
            cols = slice(h * HD, (h + 1) * HD)
            wa = jnp.broadcast_to(share_a[h : h + 1, at], (HD, slab)).T
            wb = jnp.broadcast_to(share_b[h : h + 1, at], (HD, slab)).T
            mixed = (own_ref[at, cols] * wa + from_ref[at, cols].astype(F32) * wb).astype(BF16)
            mixed_ref[at, cols] = mixed
            prod = mixed.astype(F32) * dout_ref[at, cols].astype(F32)
            stats_ref[heads + h : heads + h + 1, at] = jnp.sum(prod.T, axis=0, keepdims=True)


def backward_kernel(keys, heads, slab, first, last, *refs):
    facts_ref, *refs = refs
    n_key = len(keys)
    query_refs, dout_refs, stat_refs, refs = refs[:2], refs[2:4], refs[4:6], refs[6:]
    kv_refs, refs = refs[:n_key], refs[n_key:]
    state_refs, refs = ([], refs) if first else (refs[:1], refs[1:])
    dkv_refs, refs = refs[: n_key // 2], refs[n_key // 2 :]
    if last:
        own_ref, peer_ref, *refs = refs
    dq_ref, dk_ref, dv_ref, limit_ref, span_ref, base_ref = refs
    rows, width = 2 * slab, heads * HD
    visibility(facts_ref, limit_ref, span_ref, base_ref, slab, keys)
    if first:
        dq_ref[...] = jnp.zeros_like(dq_ref)
    else:
        dq_ref[...] = state_refs[0][...]
    dk_ref[...] = jnp.zeros_like(dk_ref)
    dv_ref[...] = jnp.zeros_like(dv_ref)

    def body(b, j, q_rows, all_rows, hidden):
        every = [slice(h * HD, (h + 1) * HD) for h in range(heads)]
        query = [query_refs[b][q_rows, cols] for cols in every]
        dout = [dout_refs[b][q_rows, cols] for cols in every]
        lse = [stat_refs[b][h : h + 1, q_rows] for h in range(heads)]
        row_dot = [stat_refs[b][heads + h : heads + h + 1, q_rows] for h in range(heads)]
        key = [kv_refs[j][:, cols] for cols in every]
        value = [kv_refs[j][:, width + h * HD : width + (h + 1) * HD] for h in range(heads)]
        scores = [dot(key[h], query[h], NT) * SCALE2 for h in range(heads)]
        weights = [jnp.exp2(scores[h] - lse[h]) for h in range(heads)]
        if hidden is not None:
            weights = [jnp.where(hidden, 0.0, weight) for weight in weights]
        d_weights = [dot(value[h], dout[h], NT) for h in range(heads)]
        d_scores = [(weights[h] * (d_weights[h] - row_dot[h])).astype(BF16) for h in range(heads)]
        add_v = [dot(weights[h].astype(BF16), dout[h], NN) for h in range(heads)]
        add_k = [dot(d_scores[h], query[h], NN) for h in range(heads)]
        add_q = [dot(key[h], d_scores[h], TN) for h in range(heads)]
        for h, cols in enumerate(every):
            dv_ref[j, :, cols] += add_v[h]
            dk_ref[j, :, cols] += add_k[h]
            dq_ref[cols, all_rows] += add_q[h]

    pairs = [(j, b) for j in range(n_key) for b in range(2)]
    for_pairs(body, limit_ref, span_ref, base_ref, slab, pairs)
    for j in range(n_key):
        at = slice(j % 2 * slab, (j % 2 + 1) * slab)
        dkv_refs[j // 2][at, :width] = (dk_ref[j] * SCALE).astype(BF16)
        dkv_refs[j // 2][at, width:] = dv_ref[j].astype(BF16)
    if not last:
        return
    for b, out_ref in enumerate((own_ref, peer_ref)):
        for s in range(2):
            at = slice((2 * b + s) * slab, (2 * b + s + 1) * slab)
            for h in range(heads):
                cols = slice(h * HD, (h + 1) * HD)
                out_ref[s * slab : (s + 1) * slab, cols] = (dq_ref[cols, at] * SCALE).T.astype(out_ref.dtype)


def grad_kernel(steps, grad_hbm, w_hbm, out_ref, grad_ref, w_ref, grad_sem, w_sem):
    tile = grad_ref.shape[2]
    copies = []
    for k in range(steps):
        at = pl.ds(k * tile, tile)
        copies.append(
            (
                pltpu.make_async_copy(grad_hbm.at[:, at], grad_ref.at[k], grad_sem.at[k]),
                pltpu.make_async_copy(w_hbm.at[:, at], w_ref.at[k], w_sem.at[k]),
            )
        )
        for copy in copies[-1]:
            copy.start()
    total = None
    for k in range(steps):
        for copy in copies[k]:
            copy.wait()
        part = dot(grad_ref[k], w_ref[k], NT)
        total = part if total is None else total + part
    out_ref[...] = total.astype(BF16)


def project_grad(grad_rows, w_out, tile):
    rows, width, steps = grad_rows.shape[0], w_out.shape[0], w_out.shape[1] // tile
    hbm = pl.BlockSpec(memory_space=pltpu.MemorySpace.HBM)
    return pl.pallas_call(
        functools.partial(grad_kernel, steps),
        out_shape=jax.ShapeDtypeStruct((rows, width), BF16),
        in_specs=[hbm, hbm],
        out_specs=VMEM,
        scratch_shapes=[
            pltpu.VMEM((steps, rows, tile), BF16),
            pltpu.VMEM((steps, width, tile), BF16),
            pltpu.SemaphoreType.DMA((steps,)),
            pltpu.SemaphoreType.DMA((steps,)),
        ],
        compiler_params=pltpu.CompilerParams(vmem_limit_bytes=20 * 2**20),
        cost_estimate=CHEAP,
        name="project_grad",
    )(in_hbm(grad_rows), in_hbm(w_out))


def out_kernel(steps, at_ref, mixed_ref, other_ref, w_hbm, w_there_hbm, out_hbm, pair_ref, w_ref, out_ref, sems):
    width, tile = mixed_ref.shape[1], w_ref.shape[2]
    loads, stores = [], []
    for k in range(steps):
        cols = pl.ds(pl.multiple_of((at_ref[0] * steps + k) * tile, tile), tile)
        pair = [
            pltpu.make_async_copy(hbm.at[:, cols], w_ref.at[k, pl.ds(part * width, width), :], sems.at[part, k])
            for part, hbm in enumerate((w_hbm, w_there_hbm))
        ]
        for load in pair:
            load.start()
        loads.append(pair)
        stores.append(
            pltpu.make_async_copy(out_ref.at[k], out_hbm.at[:, pl.ds(k * tile, tile)], sems.at[2, k])
        )
    pair_ref[:, :width] = mixed_ref[...]
    pair_ref[:, width:] = other_ref[...]
    for k in range(steps):
        for load in loads[k]:
            load.wait()
        out_ref[k] = dot(pair_ref[...], w_ref[k], NN).astype(BF16)
        stores[k].start()
    for store in stores:
        store.wait()


def project_out(core, mixed, other, w_out, w_there, tile):
    (rows, width), half = mixed.shape, w_there.shape[1] // 2
    steps = half // tile
    hbm = pl.BlockSpec(memory_space=pltpu.MemorySpace.HBM)
    return pl.pallas_call(
        functools.partial(out_kernel, steps),
        out_shape=pltpu.MemorySpace.HBM((rows, half), BF16),
        in_specs=[SMEM, VMEM, VMEM, hbm, hbm],
        out_specs=hbm,
        scratch_shapes=[
            pltpu.VMEM((rows, 2 * width), BF16),
            pltpu.VMEM((steps, 2 * width, tile), BF16),
            pltpu.VMEM((steps, rows, tile), BF16),
            pltpu.SemaphoreType.DMA((3, steps)),
        ],
        compiler_params=pltpu.CompilerParams(vmem_limit_bytes=20 * 2**20),
        cost_estimate=CHEAP,
        name="project_out",
    )(core.reshape(1).astype(jnp.int32), mixed, other, in_hbm(w_out), in_hbm(w_there))


CHEAP = pl.CostEstimate(flops=1, bytes_accessed=1, transcendentals=0)
SMEM = pl.BlockSpec(memory_space=pltpu.SMEM)
VMEM = pl.BlockSpec(memory_space=pltpu.VMEM)
LIMIT = 16 * 2**20


def add_kernel(a_ref, b_ref, out_ref):
    out_ref[...] = (a_ref[...].astype(F32) + b_ref[...].astype(F32)).astype(out_ref.dtype)


def kv_kernel(early_ref, next_ref, prev_ref, k_ref, v_ref):
    width = k_ref.shape[1]
    for out_ref, cols in ((k_ref, slice(0, width)), (v_ref, slice(width, 2 * width))):
        total = early_ref[:, cols] + next_ref[:, cols].astype(F32) + prev_ref[:, cols].astype(F32)
        out_ref[...] = total.astype(BF16)


def part_kernel(at_ref, rows_ref, out_ref):
    few = out_ref.shape[0]
    out_ref[...] = rows_ref[pl.ds(pl.multiple_of(at_ref[0] * few, few), few), :]


def out_sum_kernel(at_ref, rows_ref, from_ref, here_ref, there_ref):
    few = here_ref.shape[0]
    for out_ref, core in ((here_ref, at_ref[1]), (there_ref, 1 - at_ref[1])):
        mine = rows_ref[pl.ds(pl.multiple_of((at_ref[0] * 2 + core) * few, few), few), :]
        other = from_ref[pl.ds(pl.multiple_of(core * few, few), few), :]
        out_ref[...] = (mine.astype(F32) + other.astype(F32)).astype(BF16)


def call(kernel, outs, n_scalar, n_vector, scratch, name, flops=1, to_hbm=()):
    return pl.pallas_call(
        kernel,
        out_shape=[
            (pltpu.MemorySpace.HBM if k in to_hbm else jax.ShapeDtypeStruct)(*out) for k, out in enumerate(outs)
        ],
        in_specs=[SMEM] * n_scalar + [VMEM] * n_vector,
        out_specs=[VMEM] * len(outs),
        scratch_shapes=scratch,
        compiler_params=pltpu.CompilerParams(vmem_limit_bytes=LIMIT),
        cost_estimate=pl.CostEstimate(flops=flops, bytes_accessed=1, transcendentals=0),
        name=name,
    )


def on_device(queries, keys, values, w_out, grad_out, slab_order, frame_lengths):
    rows, width = queries.shape
    heads, slab = width // HD, rows // 2
    n_head = lax.axis_size("head")
    half = w_out.shape[1] // 2
    ctx, head = lax.axis_index("ctx"), lax.axis_index("head")
    core = head % 2

    def over_x(array, o):
        perm = [(y * 4 + x, y * 4 + (x - o) % 4) for y in range(2) for x in range(4)]
        return lax.ppermute(array, "ctx", perm)

    def over_y(array):
        return lax.ppermute(array, "ctx", [(c, (c + 4) % 8) for c in range(8)])

    def over_core(array):
        return lax.ppermute(array, "head", [(h, h ^ 1) for h in range(n_head)])

    def over_chips(array, dz, dy):
        perm = [(h, ((h // 4 + dz) % 4) * 4 + (h ^ (2 * dy)) % 4) for h in range(n_head)]
        return lax.ppermute(array, "head", perm)

    offsets = (0, 1, 3, 2)
    base = ctx // 4 * 4
    slots = [(base + (ctx + o) % 4) * 2 + s for o in offsets for s in range(2)]
    places = jnp.stack([ctx, (ctx + 4) % 8] + slots).astype(jnp.int32)
    facts = jnp.concatenate([places, slab_order, frame_lengths])
    part = (rows, width)
    stat = (8, rows)

    def masks(n_key):
        return [
            pltpu.VMEM((1, 2 * rows), jnp.int32),
            pltpu.SMEM((4, 2), jnp.int32),
            pltpu.SMEM((n_key,), jnp.int32),
        ]

    def forward(keys, pairs, state, last):
        n_key, n_query = len(keys), 1 + max(b for _, b in pairs)
        states = [((width, 2 * rows), F32), ((8, 2 * rows), F32), ((8, 2 * rows), F32)]
        results = [(part, F32), (stat, F32), (part, BF16), (stat, F32)]
        return call(
            functools.partial(forward_kernel, keys, pairs, heads, slab, not state, last),
            results if last else states,
            1,
            n_query + n_key + len(state),
            [pltpu.VMEM(*s) for s in states if last] + masks(n_key),
            "forward",
            to_hbm=(0, 1) if last else (),
        )(facts, *(queries, peer_queries)[:n_query], *(in_hbm(kv[k]) for k in keys), *state)

    def backward(keys, state, last):
        n_key, n_block = len(keys), len(keys) // 2
        states = [((width, 2 * rows), F32)]
        results = [(part, F32), (part, BF16)]
        scratch = [
            pltpu.VMEM((n_key, slab, width), F32),
            pltpu.VMEM((n_key, slab, width), F32),
        ]
        outs = call(
            functools.partial(backward_kernel, keys, heads, slab, not state, last),
            [((rows, 2 * width), BF16)] * n_block + (results if last else states),
            1,
            6 + n_key + len(state),
            [pltpu.VMEM(*s) for s in states if last] + scratch + masks(n_key),
            "backward",
            to_hbm=(0,) if last else (n_block,),
        )(
            facts,
            queries,
            peer_queries,
            grad_mixed,
            peer_grad,
            stats,
            peer_stats,
            *(in_hbm(kv[k]) for k in keys),
            *(in_hbm(array) for array in state),
        )
        return outs[:n_block], outs[n_block:]

    peer_queries = over_y(queries)
    kv = [jnp.concatenate([keys[at], values[at]], axis=1) for at in (slice(0, slab), slice(slab, rows))]
    next_0, prev_1 = over_x(kv[0], 1), over_x(kv[1], 3)
    next_1, prev_0 = over_x(kv[1], 1), over_x(kv[0], 3)
    grad_rows = lax.all_gather(grad_out, "head", axis=0, tiled=True)
    w_there = over_core(w_out)
    state = forward((0, 1), ((0, 0), (1, 0)), [], False)
    next_0, prev_1, *state = lax.optimization_barrier((next_0, prev_1, *state))
    kv += [next_0, next_1, prev_0, prev_1, over_x(next_0, 1), over_x(prev_1, 3)]
    w_there, *state = lax.optimization_barrier((w_there, *state))
    state = forward((0, 1, 2, 5), ((0, 1), (1, 1), (2, 0), (2, 1), (3, 0), (3, 1)), state, False)
    every = tuple((j, b) for j in range(2) for b in range(2))
    state = forward((3, 4), every, state, False)
    own_mixed, own_lse, peer_mixed, peer_lse = forward((6, 7), every, state, True)
    from_lse, from_mixed = over_y(peer_lse), over_y(peer_mixed)

    grad_rows, peer_lse = lax.optimization_barrier((grad_rows, peer_lse))
    grad_mixed = project_grad(grad_rows, w_out, 1024)
    peer_grad = over_y(grad_mixed)
    mixed, stats = call(
        functools.partial(merge_kernel, heads, slab),
        [(part, BF16), (stat, F32)],
        0,
        5,
        [],
        "merge",
    )(in_hbm(own_mixed), in_hbm(own_lse), from_mixed, in_hbm(from_lse), grad_mixed)
    peer_stats = over_y(stats)

    out_part = project_out(core, mixed, over_core(mixed), w_out, w_there, 512)
    z_groups = [[z * 4 + r for z in range(4)] for r in range(4)]
    out_part, peer_stats = lax.optimization_barrier((out_part, peer_stats))
    out_rows = lax.psum_scatter(
        out_part, "head", scatter_dimension=0, tiled=True, axis_index_groups=z_groups
    )

    (far_dkv,), state = backward((6, 7), [], False)
    far_dkv = over_x(far_dkv, 2)
    (next_dkv, prev_dkv), state = backward((2, 3, 4, 5), state, False)
    next_dkv, prev_dkv = over_x(next_dkv, 3), over_x(prev_dkv, 1)
    (own_dkv,), (own_dq, peer_dq) = backward((0, 1), state, True)
    peer_dq = over_y(peer_dq)

    own_dkv, far_dkv = lax.optimization_barrier((own_dkv, far_dkv))
    short = 3 * 10**8
    (kv_early,) = call(add_kernel, [((rows, 2 * width), F32)], 0, 2, [], "kv_early", short)(
        in_hbm(own_dkv), far_dkv
    )
    kv_early, next_dkv, prev_dkv = lax.optimization_barrier((kv_early, next_dkv, prev_dkv))
    k_grad, v_grad = call(kv_kernel, [(part, BF16)] * 2, 0, 3, [], "kv_sum")(kv_early, next_dkv, prev_dkv)
    own_dq, peer_dq, k_grad = lax.optimization_barrier((own_dq, peer_dq, k_grad))
    (q_grad,) = call(add_kernel, [(part, BF16)], 0, 2, [], "q_sum", short)(own_dq, peer_dq)

    few = 2 * rows // n_head // 2
    y_lo = head // 2 % 2
    spot = jnp.stack([y_lo, core]).astype(jnp.int32)
    (to_send,) = call(part_kernel, [((2 * few, half), BF16)], 1, 1, [], "out_piece")(1 - spot, in_hbm(out_rows))
    received = over_chips(to_send, 0, 1)
    received, k_grad, q_grad = lax.optimization_barrier((received, k_grad, q_grad))
    here, there = call(out_sum_kernel, [((few, half), BF16)] * 2, 1, 2, [], "out_sum")(spot, in_hbm(out_rows), received)
    there = over_core(there)
    layer_out = jnp.concatenate(
        [jnp.where(core == 0, here, there), jnp.where(core == 0, there, here)], axis=1
    )
    return layer_out, q_grad, k_grad, v_grad


def solution(mesh):
    in_specs = (
        P("ctx", "head"),
        P("ctx", "head"),
        P("ctx", "head"),
        P("head", None),
        P(("ctx", "head"), None),
        P(),
        P(),
    )
    out_specs = (P(("ctx", "head"), None), P("ctx", "head"), P("ctx", "head"), P("ctx", "head"))
    return jax.shard_map(on_device, mesh=mesh, in_specs=in_specs, out_specs=out_specs, check_vma=False)
```

```python
import functools
import math

import jax
import jax.numpy as jnp
from jax import lax
from jax.experimental import pallas as pl
from jax.experimental.pallas import tpu as pltpu
from jax.sharding import PartitionSpec as P

HD = 128
LOG2E = math.log2(math.e)
SCALE = float(HD) ** -0.5
SCALE2 = SCALE * LOG2E
START_MAX = -1e20
HIDDEN = -1e30
F32, BF16 = jnp.float32, jnp.bfloat16
NT = (((1,), (1,)), ((), ()))
TN = (((0,), (0,)), ((), ()))
NN = (((1,), (0,)), ((), ()))


def in_hbm(array):
    return pltpu.with_memory_space_constraint(array, pltpu.MemorySpace.HBM)


def dot(a, b, dims):
    return lax.dot_general(a, b, dims, preferred_element_type=F32)


def last_visible(ends, pos):
    limit = ends[-1]
    for end in reversed(ends[:-1]):
        limit = jnp.where(end > pos, end, limit)
    return limit


def visibility(facts_ref, limit_ref, span_ref, base_ref, slab, keys):
    n_slot = 8
    order, length = 2 + n_slot, 2 + n_slot + (facts_ref.shape[0] - 2 - n_slot) // 2
    ends, total = [], jnp.int32(0)
    for f in range(length, facts_ref.shape[0]):
        total = total + facts_ref[f]
        ends.append(total)
    for i in range(4):
        base = facts_ref[order + facts_ref[i // 2] * 2 + i % 2] * slab
        rows = base + lax.broadcasted_iota(jnp.int32, (1, slab), 1)
        limit_ref[:, i * slab : (i + 1) * slab] = last_visible(ends, rows)
        span_ref[i, 0] = last_visible(ends, base)
        span_ref[i, 1] = last_visible(ends, base + slab - 1)
    for j, key in enumerate(keys):
        base_ref[j] = facts_ref[order + facts_ref[2 + key]] * slab


def for_pairs(body, limit_ref, span_ref, base_ref, slab, pairs):
    for j, b in pairs:

        def step(i, carry, b=b, j=j):
            base = base_ref[j]
            low, high = span_ref[2 * b + i, 0], span_ref[2 * b + i, 1]
            q_rows = pl.ds(pl.multiple_of(i * slab, slab), slab)
            all_rows = pl.ds(pl.multiple_of((2 * b + i) * slab, slab), slab)

            @pl.when(base + slab <= low)
            def _():
                body(b, j, q_rows, all_rows, None)

            @pl.when(jnp.logical_and(base < high, base + slab > low))
            def _():
                limit = limit_ref[:, all_rows] - base
                hidden = lax.broadcasted_iota(jnp.int32, (slab, slab), 0) >= limit
                body(b, j, q_rows, all_rows, hidden)

            return carry

        lax.fori_loop(0, 2, step, 0)


def forward_kernel(keys, pairs, heads, slab, first, last, *refs):
    facts_ref, *refs = refs
    n_key = len(keys)
    n_query = 1 + max(b for _, b in pairs)
    query_refs, refs = refs[:n_query], refs[n_query:]
    kv_refs, refs = refs[:n_key], refs[n_key:]
    state_refs, refs = ([], refs) if first else (refs[:3], refs[3:])
    if last:
        own_ref, own_lse_ref, peer_ref, peer_lse_ref, *refs = refs
    acc_ref, max_ref, sum_ref, limit_ref, span_ref, base_ref = refs
    rows, width = 2 * slab, heads * HD
    visibility(facts_ref, limit_ref, span_ref, base_ref, slab, keys)
    if first:
        acc_ref[...] = jnp.zeros_like(acc_ref)
        max_ref[...] = jnp.full_like(max_ref, START_MAX)
        sum_ref[...] = jnp.zeros_like(sum_ref)
    else:
        for to_ref, from_ref in zip((acc_ref, max_ref, sum_ref), state_refs):
            to_ref[...] = from_ref[...]

    def body(b, j, q_rows, all_rows, hidden):
        every = [slice(h * HD, (h + 1) * HD) for h in range(heads)]
        key = [kv_refs[j][:, cols] for cols in every]
        value = [kv_refs[j][:, width + h * HD : width + (h + 1) * HD] for h in range(heads)]
        old = [max_ref[h : h + 1, all_rows] for h in range(heads)]
        scores = [dot(key[h], query_refs[b][q_rows, cols], NT) * SCALE2 for h, cols in enumerate(every)]
        if hidden is not None:
            scores = [jnp.where(hidden, HIDDEN, score) for score in scores]
        new = [jnp.maximum(m, jnp.max(x, axis=0, keepdims=True)) for m, x in zip(old, scores)]
        weights = [jnp.exp2(x - m) for x, m in zip(scores, new)]
        fades = [jnp.exp2(m - n) for m, n in zip(old, new)]
        sums = [
            sum_ref[h : h + 1, all_rows] * fades[h] + jnp.sum(weights[h], axis=0, keepdims=True)
            for h in range(heads)
        ]
        mixes = [dot(v, w.astype(BF16), TN) for v, w in zip(value, weights)]
        for h, cols in enumerate(every):
            max_ref[h : h + 1, all_rows] = new[h]
            sum_ref[h : h + 1, all_rows] = sums[h]
            acc_ref[cols, all_rows] = acc_ref[cols, all_rows] * fades[h] + mixes[h]

    for_pairs(body, limit_ref, span_ref, base_ref, slab, pairs)
    if not last:
        return
    total = jnp.maximum(sum_ref[...], 1e-30)
    lse = max_ref[...] + jnp.log2(total)
    own_lse_ref[...] = lse[:, :rows]
    peer_lse_ref[...] = lse[:, rows:]
    for b, out_ref in enumerate((own_ref, peer_ref)):
        for s in range(2):
            at = slice((2 * b + s) * slab, (2 * b + s + 1) * slab)
            for h in range(heads):
                cols = slice(h * HD, (h + 1) * HD)
                mixed = acc_ref[cols, at] / total[h : h + 1, at]
                out_ref[s * slab : (s + 1) * slab, cols] = mixed.T.astype(out_ref.dtype)


def merge_kernel(heads, slab, own_ref, own_lse_ref, from_ref, from_lse_ref, dout_ref, mixed_ref, stats_ref):
    a, b = own_lse_ref[...], from_lse_ref[...]
    top = jnp.maximum(a, b)
    lse = top + jnp.log2(jnp.exp2(a - top) + jnp.exp2(b - top))
    stats_ref[...] = lse
    share_a, share_b = jnp.exp2(a - lse), jnp.exp2(b - lse)
    for s in range(2):
        at = slice(s * slab, (s + 1) * slab)
        for h in range(heads):
            cols = slice(h * HD, (h + 1) * HD)
            wa = jnp.broadcast_to(share_a[h : h + 1, at], (HD, slab)).T
            wb = jnp.broadcast_to(share_b[h : h + 1, at], (HD, slab)).T
            mixed = (own_ref[at, cols] * wa + from_ref[at, cols].astype(F32) * wb).astype(BF16)
            mixed_ref[at, cols] = mixed
            prod = mixed.astype(F32) * dout_ref[at, cols].astype(F32)
            stats_ref[heads + h : heads + h + 1, at] = jnp.sum(prod.T, axis=0, keepdims=True)


def backward_kernel(keys, heads, slab, first, last, *refs):
    facts_ref, *refs = refs
    n_key = len(keys)
    query_refs, dout_refs, stat_refs, refs = refs[:2], refs[2:4], refs[4:6], refs[6:]
    kv_refs, refs = refs[:n_key], refs[n_key:]
    state_refs, refs = ([], refs) if first else (refs[:1], refs[1:])
    dkv_refs, refs = refs[: n_key // 2], refs[n_key // 2 :]
    if last:
        own_ref, peer_ref, *refs = refs
    dq_ref, dk_ref, dv_ref, limit_ref, span_ref, base_ref = refs
    rows, width = 2 * slab, heads * HD
    visibility(facts_ref, limit_ref, span_ref, base_ref, slab, keys)
    if first:
        dq_ref[...] = jnp.zeros_like(dq_ref)
    else:
        dq_ref[...] = state_refs[0][...]
    dk_ref[...] = jnp.zeros_like(dk_ref)
    dv_ref[...] = jnp.zeros_like(dv_ref)

    def body(b, j, q_rows, all_rows, hidden):
        every = [slice(h * HD, (h + 1) * HD) for h in range(heads)]
        query = [query_refs[b][q_rows, cols] for cols in every]
        dout = [dout_refs[b][q_rows, cols] for cols in every]
        lse = [stat_refs[b][h : h + 1, q_rows] for h in range(heads)]
        row_dot = [stat_refs[b][heads + h : heads + h + 1, q_rows] for h in range(heads)]
        key = [kv_refs[j][:, cols] for cols in every]
        value = [kv_refs[j][:, width + h * HD : width + (h + 1) * HD] for h in range(heads)]
        scores = [dot(key[h], query[h], NT) * SCALE2 for h in range(heads)]
        weights = [jnp.exp2(scores[h] - lse[h]) for h in range(heads)]
        if hidden is not None:
            weights = [jnp.where(hidden, 0.0, weight) for weight in weights]
        d_weights = [dot(value[h], dout[h], NT) for h in range(heads)]
        d_scores = [(weights[h] * (d_weights[h] - row_dot[h])).astype(BF16) for h in range(heads)]
        add_v = [dot(weights[h].astype(BF16), dout[h], NN) for h in range(heads)]
        add_k = [dot(d_scores[h], query[h], NN) for h in range(heads)]
        add_q = [dot(key[h], d_scores[h], TN) for h in range(heads)]
        for h, cols in enumerate(every):
            dv_ref[j, :, cols] += add_v[h]
            dk_ref[j, :, cols] += add_k[h]
            dq_ref[cols, all_rows] += add_q[h]

    pairs = [(j, b) for j in range(n_key) for b in range(2)]
    for_pairs(body, limit_ref, span_ref, base_ref, slab, pairs)
    for j in range(n_key):
        at = slice(j % 2 * slab, (j % 2 + 1) * slab)
        dkv_refs[j // 2][at, :width] = (dk_ref[j] * SCALE).astype(BF16)
        dkv_refs[j // 2][at, width:] = dv_ref[j].astype(BF16)
    if not last:
        return
    for b, out_ref in enumerate((own_ref, peer_ref)):
        for s in range(2):
            at = slice((2 * b + s) * slab, (2 * b + s + 1) * slab)
            for h in range(heads):
                cols = slice(h * HD, (h + 1) * HD)
                out_ref[s * slab : (s + 1) * slab, cols] = (dq_ref[cols, at] * SCALE).T.astype(out_ref.dtype)


def grad_kernel(steps, grad_hbm, w_hbm, out_ref, grad_ref, w_ref, grad_sem, w_sem):
    tile = grad_ref.shape[2]
    copies = []
    for k in range(steps):
        at = pl.ds(k * tile, tile)
        copies.append(
            (
                pltpu.make_async_copy(grad_hbm.at[:, at], grad_ref.at[k], grad_sem.at[k]),
                pltpu.make_async_copy(w_hbm.at[:, at], w_ref.at[k], w_sem.at[k]),
            )
        )
        for copy in copies[-1]:
            copy.start()
    total = None
    for k in range(steps):
        for copy in copies[k]:
            copy.wait()
        part = dot(grad_ref[k], w_ref[k], NT)
        total = part if total is None else total + part
    out_ref[...] = total.astype(BF16)


def project_grad(grad_rows, w_out, tile):
    rows, width, steps = grad_rows.shape[0], w_out.shape[0], w_out.shape[1] // tile
    hbm = pl.BlockSpec(memory_space=pltpu.MemorySpace.HBM)
    return pl.pallas_call(
        functools.partial(grad_kernel, steps),
        out_shape=jax.ShapeDtypeStruct((rows, width), BF16),
        in_specs=[hbm, hbm],
        out_specs=VMEM,
        scratch_shapes=[
            pltpu.VMEM((steps, rows, tile), BF16),
            pltpu.VMEM((steps, width, tile), BF16),
            pltpu.SemaphoreType.DMA((steps,)),
            pltpu.SemaphoreType.DMA((steps,)),
        ],
        compiler_params=pltpu.CompilerParams(vmem_limit_bytes=20 * 2**20),
        cost_estimate=CHEAP,
        name="project_grad",
    )(in_hbm(grad_rows), in_hbm(w_out))


def out_kernel(steps, at_ref, mixed_ref, other_ref, w_hbm, w_there_hbm, out_hbm, pair_ref, w_ref, out_ref, sems):
    width, tile = mixed_ref.shape[1], w_ref.shape[2]
    loads, stores = [], []
    for k in range(steps):
        cols = pl.ds(pl.multiple_of((at_ref[0] * steps + k) * tile, tile), tile)
        pair = [
            pltpu.make_async_copy(hbm.at[:, cols], w_ref.at[k, pl.ds(part * width, width), :], sems.at[part, k])
            for part, hbm in enumerate((w_hbm, w_there_hbm))
        ]
        for load in pair:
            load.start()
        loads.append(pair)
        stores.append(
            pltpu.make_async_copy(out_ref.at[k], out_hbm.at[:, pl.ds(k * tile, tile)], sems.at[2, k])
        )
    pair_ref[:, :width] = mixed_ref[...]
    pair_ref[:, width:] = other_ref[...]
    for k in range(steps):
        for load in loads[k]:
            load.wait()
        out_ref[k] = dot(pair_ref[...], w_ref[k], NN).astype(BF16)
        stores[k].start()
    for store in stores:
        store.wait()


def project_out(core, mixed, other, w_out, w_there, tile):
    (rows, width), half = mixed.shape, w_there.shape[1] // 2
    steps = half // tile
    hbm = pl.BlockSpec(memory_space=pltpu.MemorySpace.HBM)
    return pl.pallas_call(
        functools.partial(out_kernel, steps),
        out_shape=pltpu.MemorySpace.HBM((rows, half), BF16),
        in_specs=[SMEM, VMEM, VMEM, hbm, hbm],
        out_specs=hbm,
        scratch_shapes=[
            pltpu.VMEM((rows, 2 * width), BF16),
            pltpu.VMEM((steps, 2 * width, tile), BF16),
            pltpu.VMEM((steps, rows, tile), BF16),
            pltpu.SemaphoreType.DMA((3, steps)),
        ],
        compiler_params=pltpu.CompilerParams(vmem_limit_bytes=20 * 2**20),
        cost_estimate=CHEAP,
        name="project_out",
    )(core.reshape(1).astype(jnp.int32), mixed, other, in_hbm(w_out), in_hbm(w_there))


CHEAP = pl.CostEstimate(flops=1, bytes_accessed=1, transcendentals=0)
SMEM = pl.BlockSpec(memory_space=pltpu.SMEM)
VMEM = pl.BlockSpec(memory_space=pltpu.VMEM)
LIMIT = 16 * 2**20


def add_kernel(a_ref, b_ref, out_ref):
    out_ref[...] = (a_ref[...].astype(F32) + b_ref[...].astype(F32)).astype(out_ref.dtype)


def kv_kernel(early_ref, next_ref, prev_ref, k_ref, v_ref):
    width = k_ref.shape[1]
    for out_ref, cols in ((k_ref, slice(0, width)), (v_ref, slice(width, 2 * width))):
        total = early_ref[:, cols] + next_ref[:, cols].astype(F32) + prev_ref[:, cols].astype(F32)
        out_ref[...] = total.astype(BF16)


def part_kernel(at_ref, rows_ref, out_ref):
    few = out_ref.shape[0]
    out_ref[...] = rows_ref[pl.ds(pl.multiple_of(at_ref[0] * few, few), few), :]


def out_sum_kernel(at_ref, rows_ref, from_ref, here_ref, there_ref):
    few = here_ref.shape[0]
    for out_ref, core in ((here_ref, at_ref[1]), (there_ref, 1 - at_ref[1])):
        mine = rows_ref[pl.ds(pl.multiple_of((at_ref[0] * 2 + core) * few, few), few), :]
        other = from_ref[pl.ds(pl.multiple_of(core * few, few), few), :]
        out_ref[...] = (mine.astype(F32) + other.astype(F32)).astype(BF16)


def call(kernel, outs, n_scalar, n_vector, scratch, name, flops=1):
    return pl.pallas_call(
        kernel,
        out_shape=[jax.ShapeDtypeStruct(shape, dtype) for shape, dtype in outs],
        in_specs=[SMEM] * n_scalar + [VMEM] * n_vector,
        out_specs=[VMEM] * len(outs),
        scratch_shapes=scratch,
        compiler_params=pltpu.CompilerParams(vmem_limit_bytes=LIMIT),
        cost_estimate=pl.CostEstimate(flops=flops, bytes_accessed=1, transcendentals=0),
        name=name,
    )


def on_device(queries, keys, values, w_out, grad_out, slab_order, frame_lengths):
    rows, width = queries.shape
    heads, slab = width // HD, rows // 2
    n_head = lax.axis_size("head")
    half = w_out.shape[1] // 2
    ctx, head = lax.axis_index("ctx"), lax.axis_index("head")
    core = head % 2

    def over_x(array, o):
        perm = [(y * 4 + x, y * 4 + (x - o) % 4) for y in range(2) for x in range(4)]
        return lax.ppermute(array, "ctx", perm)

    def over_y(array):
        return lax.ppermute(array, "ctx", [(c, (c + 4) % 8) for c in range(8)])

    def over_core(array):
        return lax.ppermute(array, "head", [(h, h ^ 1) for h in range(n_head)])

    def over_chips(array, dz, dy):
        perm = [(h, ((h // 4 + dz) % 4) * 4 + (h ^ (2 * dy)) % 4) for h in range(n_head)]
        return lax.ppermute(array, "head", perm)

    offsets = (0, 1, 3, 2)
    base = ctx // 4 * 4
    slots = [(base + (ctx + o) % 4) * 2 + s for o in offsets for s in range(2)]
    places = jnp.stack([ctx, (ctx + 4) % 8] + slots).astype(jnp.int32)
    facts = jnp.concatenate([places, slab_order, frame_lengths])
    part = (rows, width)
    stat = (8, rows)

    def masks(n_key):
        return [
            pltpu.VMEM((1, 2 * rows), jnp.int32),
            pltpu.SMEM((4, 2), jnp.int32),
            pltpu.SMEM((n_key,), jnp.int32),
        ]

    def forward(keys, pairs, state, last):
        n_key, n_query = len(keys), 1 + max(b for _, b in pairs)
        states = [((width, 2 * rows), F32), ((8, 2 * rows), F32), ((8, 2 * rows), F32)]
        results = [(part, F32), (stat, F32), (part, BF16), (stat, F32)]
        return call(
            functools.partial(forward_kernel, keys, pairs, heads, slab, not state, last),
            results if last else states,
            1,
            n_query + n_key + len(state),
            [pltpu.VMEM(*s) for s in states if last] + masks(n_key),
            "forward",
        )(facts, *(queries, peer_queries)[:n_query], *(in_hbm(kv[k]) for k in keys), *state)

    def backward(keys, state, last):
        n_key, n_block = len(keys), len(keys) // 2
        states = [((width, 2 * rows), F32)]
        results = [(part, F32), (part, BF16)]
        scratch = [
            pltpu.VMEM((n_key, slab, width), F32),
            pltpu.VMEM((n_key, slab, width), F32),
        ]
        outs = call(
            functools.partial(backward_kernel, keys, heads, slab, not state, last),
            [((rows, 2 * width), BF16)] * n_block + (results if last else states),
            1,
            6 + n_key + len(state),
            [pltpu.VMEM(*s) for s in states if last] + scratch + masks(n_key),
            "backward",
        )(
            facts,
            queries,
            peer_queries,
            grad_mixed,
            peer_grad,
            stats,
            peer_stats,
            *(in_hbm(kv[k]) for k in keys),
            *(in_hbm(array) for array in state),
        )
        return outs[:n_block], outs[n_block:]

    peer_queries = over_y(queries)
    kv = [jnp.concatenate([keys[at], values[at]], axis=1) for at in (slice(0, slab), slice(slab, rows))]
    next_0, prev_1 = over_x(kv[0], 1), over_x(kv[1], 3)
    next_1, prev_0 = over_x(kv[1], 1), over_x(kv[0], 3)
    grad_rows = lax.all_gather(grad_out, "head", axis=0, tiled=True)
    w_there = over_core(w_out)
    state = forward((0, 1), ((0, 0), (1, 0)), [], False)
    next_0, prev_1, *state = lax.optimization_barrier((next_0, prev_1, *state))
    kv += [next_0, next_1, prev_0, prev_1, over_x(next_0, 1), over_x(prev_1, 3)]
    w_there, *state = lax.optimization_barrier((w_there, *state))
    state = forward((0, 1, 2, 5), ((0, 1), (1, 1), (2, 0), (2, 1), (3, 0), (3, 1)), state, False)
    every = tuple((j, b) for j in range(2) for b in range(2))
    state = forward((3, 4), every, state, False)
    own_mixed, own_lse, peer_mixed, peer_lse = forward((6, 7), every, state, True)
    from_lse, from_mixed = over_y(peer_lse), over_y(peer_mixed)

    grad_rows, peer_lse = lax.optimization_barrier((grad_rows, peer_lse))
    grad_mixed = project_grad(grad_rows, w_out, 1024)
    peer_grad = over_y(grad_mixed)
    mixed, stats = call(
        functools.partial(merge_kernel, heads, slab),
        [(part, BF16), (stat, F32)],
        0,
        5,
        [],
        "merge",
    )(in_hbm(own_mixed), in_hbm(own_lse), from_mixed, in_hbm(from_lse), grad_mixed)
    peer_stats = over_y(stats)

    out_part = project_out(core, mixed, over_core(mixed), w_out, w_there, 1024)
    z_groups = [[z * 4 + r for z in range(4)] for r in range(4)]
    out_part, peer_grad, peer_stats = lax.optimization_barrier((out_part, peer_grad, peer_stats))
    out_rows = lax.psum_scatter(
        out_part, "head", scatter_dimension=0, tiled=True, axis_index_groups=z_groups
    )

    (far_dkv,), state = backward((6, 7), [], False)
    far_dkv = over_x(far_dkv, 2)
    (next_dkv, prev_dkv), state = backward((2, 3, 4, 5), state, False)
    next_dkv, prev_dkv = over_x(next_dkv, 3), over_x(prev_dkv, 1)
    (own_dkv,), (own_dq, peer_dq) = backward((0, 1), state, True)
    peer_dq = over_y(peer_dq)

    own_dkv, far_dkv = lax.optimization_barrier((own_dkv, far_dkv))
    short = 3 * 10**8
    (kv_early,) = call(add_kernel, [((rows, 2 * width), F32)], 0, 2, [], "kv_early", short)(
        in_hbm(own_dkv), far_dkv
    )
    kv_early, next_dkv, prev_dkv = lax.optimization_barrier((kv_early, next_dkv, prev_dkv))
    k_grad, v_grad = call(kv_kernel, [(part, BF16)] * 2, 0, 3, [], "kv_sum")(kv_early, next_dkv, prev_dkv)
    own_dq, peer_dq, k_grad = lax.optimization_barrier((own_dq, peer_dq, k_grad))
    (q_grad,) = call(add_kernel, [(part, BF16)], 0, 2, [], "q_sum", short)(own_dq, peer_dq)

    few = 2 * rows // n_head // 2
    y_lo = head // 2 % 2
    spot = jnp.stack([y_lo, core]).astype(jnp.int32)
    (to_send,) = call(part_kernel, [((2 * few, half), BF16)], 1, 1, [], "out_piece")(1 - spot, in_hbm(out_rows))
    received = over_chips(to_send, 0, 1)
    received, k_grad, q_grad = lax.optimization_barrier((received, k_grad, q_grad))
    here, there = call(out_sum_kernel, [((few, half), BF16)] * 2, 1, 2, [], "out_sum")(spot, in_hbm(out_rows), received)
    there = over_core(there)
    layer_out = jnp.concatenate(
        [jnp.where(core == 0, here, there), jnp.where(core == 0, there, here)], axis=1
    )
    return layer_out, q_grad, k_grad, v_grad


def solution(mesh):
    in_specs = (
        P("ctx", "head"),
        P("ctx", "head"),
        P("ctx", "head"),
        P("head", None),
        P(("ctx", "head"), None),
        P(),
        P(),
    )
    out_specs = (P(("ctx", "head"), None), P("ctx", "head"), P("ctx", "head"), P("ctx", "head"))
    return jax.shard_map(on_device, mesh=mesh, in_specs=in_specs, out_specs=out_specs, check_vma=False)
```
